32 devices in a mesh: groups: 2 (over y), seq: 8 (over z, x), tensor: 2 (over core).
Axes of the slice: x: 2, y: 2, z: 4, core: 2. Of those that a mesh axis runs over, the one named last changes fastest.
Arguments:
- queries: bfloat16 [4096, 2048], P(('groups', 'seq', 'tensor')), parts along dimension 0, may hold values from -80 to 80
- keys: bfloat16 [4096, 1024], P(('groups', 'seq', 'tensor')), parts along dimension 0, may hold values from -4 to 4
- values: bfloat16 [4096, 1024], P(('groups', 'seq', 'tensor')), parts along dimension 0, may hold values from -6 to 6
- block_lists: int32 [16, 32, 12], P(('seq', 'tensor')), may hold values from 0 to 31, as said below
Outputs:
- attended: bfloat16 [4096, 2048], P(('groups', 'seq', 'tensor')), parts along dimension 0
The draws below stay inside these ranges and needn't reach their ends.
There are 2 independent parts, one for each index of `groups`. The reference program is written for one: setup_inputs(seed, part) draws one part's arguments, and reference() takes and returns one part's arrays. A program takes and returns all parts, laid end to end along the dimension named above; an argument that names none is the same for every part. Nothing has to cross between parts.
Inputs may be any that keep to these rules, and one draw needn't show every extreme that they name: `block_lists`: for head h and query block b, slot 0 is b; slots 0 to min(b + 1, 12) - 1 hold distinct blocks at most b; later slots equal b.
All inputs are finite; a program needn't handle non-finite values.
Results may differ from the reference program's by a relative error of at most 0.0041.
Values may be sent and summed in bfloat16 or wider, within the bound.
A program may use at most 128 MiB of HBM per device.

```python
import jax
import jax.numpy as jnp
from jax import lax

HD = 128
KVH = 8
BLK = 64
KSEL = 12
QG = 16
H = 16
TOKENS = 2048
NQB = 32


def shared_keys(key):
    base = jax.random.normal(key, (TOKENS, KVH * HD), jnp.float32)
    return jnp.clip(base, -4.0, 4.0)


def draw_keys(key, part):
    base = shared_keys(key)
    return base.astype(jnp.bfloat16)


def draw_queries(key, part):
    key = jax.random.fold_in(key, 7)
    fresh = jax.random.normal(key, (TOKENS, H * HD), jnp.float32)
    fresh = jnp.clip(fresh, -6.0, 6.0)
    return fresh.astype(jnp.bfloat16)


def draw_block_lists(key, part):
    key = jax.random.fold_in(key, 11)
    key_a, key_b, key_c = jax.random.split(key, 3)
    verts = jax.random.randint(key_a, (H, 4), 0, NQB)
    slashes = jax.random.randint(key_b, (H, 4), 1, 9)
    noise = jax.random.randint(key_c, (H, NQB, NQB), 0, 64)
    qb = jnp.arange(NQB, dtype=jnp.int32)[None, :, None]
    kb = jnp.arange(NQB, dtype=jnp.int32)[None, None, :]
    is_vert = jnp.any(kb[..., None] == verts[:, None, None, :], axis=-1)
    is_slash = jnp.any((qb - kb)[..., None] == slashes[:, None, None, :], axis=-1)
    score = noise + 128 * is_vert.astype(jnp.int32) + 128 * is_slash.astype(jnp.int32)
    score = jnp.where(kb == qb, 1024, score)
    score = jnp.where(kb > qb, -1, score)
    score = score * NQB + kb
    picked = jax.lax.top_k(score, KSEL)[1].astype(jnp.int32)
    slot = jnp.arange(KSEL, dtype=jnp.int32)[None, None, :]
    qfull = jnp.broadcast_to(jnp.arange(NQB, dtype=jnp.int32)[None, :, None], picked.shape)
    return jnp.where(slot <= qfull, picked, qfull)


def level_of(rng, extent, shards, least, largest):
    level, own = 1.0, jax.random.fold_in(rng, 6)
    for position, parts in shards:
        steps = jnp.exp(jax.random.uniform(jax.random.fold_in(own, position), (parts,), jnp.float32, least / len(shards), largest / len(shards)))
        level = level * jnp.repeat(steps, extent[position] // parts).reshape([-1 if axis == position else 1 for axis in range(len(extent))])
    return level


def bell_draw(stream_key, dims, width, reach, shards=(), kind=jnp.bfloat16):
    gain = level_of(stream_key, dims, shards, -0.22, 0.18) if shards else 1.0
    entries = jax.random.normal(stream_key, dims, jnp.float32) * width * gain
    return jnp.minimum(jnp.maximum(entries, -reach), reach).astype(kind)


def setup_inputs(seed: int = 0, part: int = 0) -> dict:
    streams_of = jax.random.split(jax.random.key(seed), 5)
    own_keys = jax.random.split(jax.random.fold_in(streams_of[4], part), 5)
    return {
        "queries": draw_queries(jax.random.fold_in(jax.random.fold_in(streams_of[4], part), 71), part),
        "keys": draw_keys(jax.random.fold_in(jax.random.fold_in(streams_of[4], part), 71), part),
        "values": bell_draw(own_keys[2], (TOKENS, KVH * HD), 1.0, 6.0, ((0, 16),)),
        "block_lists": draw_block_lists(jax.random.fold_in(streams_of[4], 71), part),
    }


def attend_group(qblk, kfull, vfull, lists, first):
    kblk = kfull[lists].astype(jnp.float32)
    vblk = vfull[lists].astype(jnp.float32)
    scores = jnp.einsum('gid,gsjd->gisj', qblk.astype(jnp.float32), kblk) / jnp.sqrt(jnp.float32(HD))
    qidx = first + jnp.arange(lists.shape[0], dtype=jnp.int32)
    qpos = qidx[:, None] * BLK + jnp.arange(BLK, dtype=jnp.int32)[None, :]
    kpos = lists[:, :, None] * BLK + jnp.arange(BLK, dtype=jnp.int32)[None, None, :]
    slot_live = jnp.arange(KSEL, dtype=jnp.int32)[None, :] < jnp.minimum(qidx + 1, KSEL)[:, None]
    valid = (kpos[:, None, :, :] <= qpos[:, :, None, None]) & slot_live[:, None, :, None]
    masked = jnp.where(valid, scores, jnp.float32(-1e+30))
    top = lax.optimization_barrier(jnp.max(masked, axis=(2, 3), keepdims=True))
    probs = jnp.where(valid, jnp.exp(masked - top), jnp.float32(0.0))
    total = lax.optimization_barrier(jnp.sum(probs, axis=(2, 3)))
    weights = probs.astype(jnp.bfloat16)
    summed = jnp.einsum('gisj,gsjd->gid', weights.astype(jnp.float32), vblk)
    return (summed / total[:, :, None]).astype(jnp.bfloat16)

def one_head(qhead, khead, vhead, lists):
    groups = NQB // QG
    qgrp = qhead.reshape(groups, QG, BLK, HD)
    lgrp = lists.reshape(groups, QG, KSEL)
    firsts = jnp.arange(groups, dtype=jnp.int32) * QG
    kfull = khead.reshape(NQB, BLK, HD)
    vfull = vhead.reshape(NQB, BLK, HD)
    result = lax.map(lambda item: attend_group(item[0], kfull, vfull, item[1], item[2]), (qgrp, lgrp, firsts))
    return result.reshape(TOKENS, HD)

def reference(queries, keys, values, block_lists):
    ratio = H // KVH
    q3 = queries.reshape(TOKENS, H, HD)
    k3 = keys.reshape(TOKENS, KVH, HD)
    v3 = values.reshape(TOKENS, KVH, HD)

    def per_head(head):
        group = head // ratio
        qhead = lax.dynamic_index_in_dim(q3, head, 1, keepdims=False)
        khead = lax.dynamic_index_in_dim(k3, group, 1, keepdims=False)
        vhead = lax.dynamic_index_in_dim(v3, group, 1, keepdims=False)
        lists = lax.dynamic_index_in_dim(block_lists, head, 0, keepdims=False)
        return one_head(qhead, khead, vhead, lists)
    outs = lax.map(per_head, jnp.arange(H, dtype=jnp.int32))
    return jnp.transpose(outs, (1, 0, 2)).reshape(TOKENS, H * HD)
```

```python
import functools

import jax
import jax.numpy as jnp
from jax import lax
from jax.experimental import pallas as pl
from jax.experimental.pallas import tpu as pltpu
from jax.sharding import PartitionSpec as P

HD = 128
BLK = 64
KSEL = 12
MESH = pl.DeviceIdType.MESH
COEF = 1.4426950408889634 / (128.0**0.5)


def attend_block(qblk, kcat, vcat, block):
    raw = lax.dot_general(qblk, kcat, (((1,), (1,)), ((), ())), preferred_element_type=jnp.float32)
    row = lax.broadcasted_iota(jnp.int32, raw.shape, 0)
    col = lax.broadcasted_iota(jnp.int32, raw.shape, 1)
    live = jnp.minimum(block + 1, KSEL) * BLK
    keep = ((col >= BLK) | (col <= row)) & (col < live)
    raw = jnp.where(keep, raw, jnp.float32(-1e30))
    top = jnp.max(raw, axis=1, keepdims=True)
    probs = jnp.exp2((raw - top) * jnp.float32(COEF))
    total = jnp.sum(probs, axis=1, keepdims=True)
    summed = jnp.dot(probs.astype(jnp.bfloat16), vcat, preferred_element_type=jnp.float32)
    return (summed / total).astype(jnp.bfloat16)


def kernel(nc, nt, ratio, mult, lists, q, k, v, out, qh, kv, oh,
           s_kv, s_q, s_o, s_f, s_s, l_kv, l_o, r_kv, r_f, r_s, r_q, r_o):
    n = nc * nt
    rows = q.shape[0]
    per = rows // BLK
    c, t = lax.axis_index("seq"), lax.axis_index("tensor")
    me = c * nt + t
    sib = 1 - t

    def dev(chip, core):
        return {"seq": chip, "tensor": core}

    def part(index):
        return pl.ds(pl.multiple_of(index * rows, rows), rows)

    def blocks(index):
        return pl.ds(index * per, per)

    def cols(head):
        return pl.ds(pl.multiple_of(head * HD, HD), HD)

    def remote(src, dst, send, recv, chip, core):
        return pltpu.make_async_remote_copy(
            src_ref=src, dst_ref=dst, send_sem=send, recv_sem=recv,
            device_id=dev(chip, core), device_id_type=MESH,
        )

    def drain(ref, sem):
        pltpu.make_async_copy(ref, ref, sem).wait()

    def loop(start, stop, step):
        def run(i, _):
            step(i)
            return 0
        lax.fori_loop(start, stop, run, 0)

    barrier = pltpu.get_barrier_semaphore()

    def greet(i):
        p = lax.rem(me + i, n)
        pl.semaphore_signal(barrier, inc=1, device_id=dev(p // nt, lax.rem(p, nt)), device_id_type=MESH)

    loop(1, n, greet)
    pl.semaphore_wait(barrier, n - 1)

    def send_kv(j):
        dc = lax.rem(c + j * mult, nc)
        head = cols((dc * nt) // ratio)
        for core, src in ((0, k), (1, v)):
            remote(src.at[:, :, head], kv.at[core, blocks(me)], s_kv, r_kv.at[me], dc, core).start()

    loop(1, nc, send_kv)
    head = cols(me // ratio)
    local = []
    for core, src in ((0, k), (1, v)):
        remote(src.at[:, :, head], kv.at[core, blocks(me)], s_s.at[core], r_s.at[core], c, sib).start()
        local.append(pltpu.make_async_copy(src.at[:, :, head], kv.at[core, blocks(me)], l_kv.at[core]))
        local[-1].start()

    pltpu.make_async_copy(q.at[:, cols(me)], qh.at[part(me)], r_q.at[me]).start()
    remote(q.at[:, cols(c * nt + sib)], qh.at[part(me)], s_q, r_q.at[me], c, sib).start()

    def send_q(j):
        dc = lax.rem(c + j * mult, nc)
        for core in range(nt):
            remote(q.at[:, cols(dc * nt + core)], qh.at[part(me)], s_q, r_q.at[me], dc, core).start()

    loop(1, nc, send_q)

    def forward(j):
        sc = lax.rem(c + (nc - j) * mult, nc)
        for core in range(nt):
            s = sc * nt + core
            drain(kv.at[t, blocks(s)], r_kv.at[s])
            remote(kv.at[t, blocks(s)], kv.at[t, blocks(s)], s_f, r_f, c, sib).start()

    loop(1, nc, forward)
    for core in range(nt):
        local[core].wait()
        drain(kv.at[core, blocks(0)], r_s.at[core])
    drain(kv.at[0, pl.ds(0, (n - nt) * per)], r_f)

    def attend(i):
        j = i // nt
        sc = lax.rem(c + (nc - j) * mult, nc)
        score = lax.rem(t + i, nt)
        s = sc * nt + score
        drain(qh.at[part(s)], r_q.at[s])
        for inner in range(per):
            block = s * per + inner
            listed = [lists[block * KSEL + slot] for slot in range(KSEL)]
            kcat = jnp.concatenate([kv[0, i] for i in listed], axis=0)
            vcat = jnp.concatenate([kv[1, i] for i in listed], axis=0)
            here = pl.ds(pl.multiple_of(block * BLK, BLK), BLK)
            oh[here, :] = attend_block(qh[here, :], kcat, vcat, block)

        @pl.when(i == 0)
        def _():
            pltpu.make_async_copy(oh.at[part(s)], out.at[:, cols(me)], l_o).start()

        @pl.when(i > 0)
        def _():
            remote(oh.at[part(s)], out.at[:, cols(me)], s_o, r_o, sc, score).start()

    loop(0, n, attend)

    drain(oh.at[part(0)], l_o)
    others = pl.ds(0, (n - 1) * HD)
    drain(out.at[:, others], r_o)
    drain(out.at[:, others], s_o)
    drain(out.at[:, others], s_q)
    drain(kv.at[0, pl.ds(0, (n - nt) * per)], s_kv)
    drain(kv.at[0, pl.ds(0, (n - nt) * per)], s_f)
    for core in range(nt):
        drain(kv.at[core, blocks(0)], s_s.at[core])


def body(nc, nt, queries, keys, values, block_lists):
    rows, width = queries.shape
    n = nc * nt
    heads = width // HD
    kv_heads = keys.shape[1] // HD
    ratio = heads // kv_heads
    assert nt == 2 and heads == n and ratio % nt == 0 and rows % BLK == 0
    mult = nc // 2 - 1 if nc >= 4 and nc & (nc - 1) == 0 else 1
    dma, shape = pltpu.SemaphoreType.DMA, jax.ShapeDtypeStruct
    hbm = pl.BlockSpec(memory_space=pl.ANY)
    return pl.pallas_call(
        functools.partial(kernel, nc, nt, ratio, mult),
        out_shape=shape((rows, width), jnp.bfloat16),
        in_specs=[pl.BlockSpec(memory_space=pltpu.SMEM), hbm, hbm, hbm],
        out_specs=hbm,
        scratch_shapes=[
            pltpu.VMEM((n * rows, HD), jnp.bfloat16),
            pltpu.VMEM((2, n * rows // BLK, BLK, HD), jnp.bfloat16),
            pltpu.VMEM((n * rows, HD), jnp.bfloat16),
            dma, dma, dma, dma, dma((nt,)), dma((nt,)), dma,
            dma((n,)), dma, dma((nt,)), dma((n,)), dma,
        ],
        compiler_params=pltpu.CompilerParams(
            collective_id=0, has_side_effects=True, vmem_limit_bytes=40 * 2**20
        ),
        cost_estimate=pl.CostEstimate(
            flops=4 * n * rows * KSEL * BLK * HD, bytes_accessed=8 * n * rows * HD, transcendentals=n * rows * KSEL * BLK
        ),
    )(
        block_lists.reshape(-1),
        queries,
        keys.reshape(rows // BLK, BLK, kv_heads * HD),
        values.reshape(rows // BLK, BLK, kv_heads * HD),
    )


def solution(mesh):
    placed = (
        P(("groups", "seq", "tensor"), None),
        P(("groups", "seq", "tensor"), None),
        P(("groups", "seq", "tensor"), None),
        P(("seq", "tensor"), None, None),
    )
    return jax.shard_map(
        functools.partial(body, mesh.shape["seq"], mesh.shape["tensor"]),
        mesh=mesh,
        in_specs=placed,
        out_specs=P(("groups", "seq", "tensor"), None),
        check_vma=False,
    )
```

```python
import functools

import jax
import jax.numpy as jnp
from jax import lax
from jax.experimental import pallas as pl
from jax.experimental.pallas import tpu as pltpu
from jax.sharding import PartitionSpec as P

HD = 128
BLK = 64
KSEL = 12
VMEM_MIB = 60
MESH = pl.DeviceIdType.MESH
COEF = 1.4426950408889634 / (128.0**0.5)


def attend_block(qblk, kcat, vcat, block):
    raw = lax.dot_general(qblk, kcat, (((1,), (1,)), ((), ())), preferred_element_type=jnp.float32)
    row = lax.broadcasted_iota(jnp.int32, raw.shape, 0)
    col = lax.broadcasted_iota(jnp.int32, raw.shape, 1)
    live = jnp.minimum(block + 1, KSEL) * BLK
    keep = ((col >= BLK) | (col <= row)) & (col < live)
    raw = jnp.where(keep, raw, jnp.float32(-1e30))
    top = jnp.max(raw, axis=1, keepdims=True)
    probs = jnp.exp2((raw - top) * jnp.float32(COEF))
    total = jnp.sum(probs, axis=1, keepdims=True)
    summed = jnp.dot(probs.astype(jnp.bfloat16), vcat, preferred_element_type=jnp.float32)
    return (summed / total).astype(jnp.bfloat16)


def kernel(nc, nt, ratio, mult, lists, q, k, v, out, qh, kv, oh,
           s_kv, s_q, s_o, s_f, s_s, l_kv, l_o, r_kv, r_f, r_s, r_q, r_o):
    n = nc * nt
    rows = q.shape[0]
    per = rows // BLK
    c, t = lax.axis_index("seq"), lax.axis_index("tensor")
    me = c * nt + t
    sib = 1 - t

    def dev(chip, core):
        return {"seq": chip, "tensor": core}

    def part(index):
        return pl.ds(pl.multiple_of(index * rows, rows), rows)

    def blocks(index):
        return pl.ds(index * per, per)

    def cols(head):
        return pl.ds(pl.multiple_of(head * HD, HD), HD)

    def remote(src, dst, send, recv, chip, core):
        return pltpu.make_async_remote_copy(
            src_ref=src, dst_ref=dst, send_sem=send, recv_sem=recv,
            device_id=dev(chip, core), device_id_type=MESH,
        )

    def drain(ref, sem):
        pltpu.make_async_copy(ref, ref, sem).wait()

    def loop(start, stop, step):
        def run(i, _):
            step(i)
            return 0
        lax.fori_loop(start, stop, run, 0)

    barrier = pltpu.get_barrier_semaphore()

    def greet(i):
        p = lax.rem(me + i, n)
        pl.semaphore_signal(barrier, inc=1, device_id=dev(p // nt, lax.rem(p, nt)), device_id_type=MESH)

    loop(1, n, greet)
    pl.semaphore_wait(barrier, n - 1)

    def send_kv(j):
        dc = lax.rem(c + j * mult, nc)
        head = cols((dc * nt) // ratio)
        for core, src in ((0, k), (1, v)):
            remote(src.at[:, :, head], kv.at[core, blocks(me)], s_kv, r_kv.at[me], dc, core).start()

    loop(1, nc, send_kv)
    head = cols(me // ratio)
    local = []
    for core, src in ((0, k), (1, v)):
        remote(src.at[:, :, head], kv.at[core, blocks(me)], s_s.at[core], r_s.at[core], c, sib).start()
        local.append(pltpu.make_async_copy(src.at[:, :, head], kv.at[core, blocks(me)], l_kv.at[core]))
        local[-1].start()

    pltpu.make_async_copy(q.at[:, cols(me)], qh.at[part(me)], r_q.at[me]).start()
    remote(q.at[:, cols(c * nt + sib)], qh.at[part(me)], s_q, r_q.at[me], c, sib).start()

    def send_q(j):
        dc = lax.rem(c + j * mult, nc)
        for core in range(nt):
            remote(q.at[:, cols(dc * nt + core)], qh.at[part(me)], s_q, r_q.at[me], dc, core).start()

    loop(1, nc, send_q)

    def forward(j):
        sc = lax.rem(c + (nc - j) * mult, nc)
        for core in range(nt):
            s = sc * nt + core
            drain(kv.at[t, blocks(s)], r_kv.at[s])
            remote(kv.at[t, blocks(s)], kv.at[t, blocks(s)], s_f, r_f, c, sib).start()

    loop(1, nc, forward)
    for core in range(nt):
        local[core].wait()
        drain(kv.at[core, blocks(0)], r_s.at[core])
    drain(kv.at[0, pl.ds(0, (n - nt) * per)], r_f)

    def attend(i):
        j = i // nt
        sc = lax.rem(c + (nc - j) * mult, nc)
        score = lax.rem(t + i, nt)
        s = sc * nt + score
        drain(qh.at[part(s)], r_q.at[s])
        for inner in range(per):
            block = s * per + inner
            listed = [lists[block * KSEL + slot] for slot in range(KSEL)]
            kcat = jnp.concatenate([kv[0, i] for i in listed], axis=0)
            vcat = jnp.concatenate([kv[1, i] for i in listed], axis=0)
            here = pl.ds(pl.multiple_of(block * BLK, BLK), BLK)
            oh[here, :] = attend_block(qh[here, :], kcat, vcat, block)

        @pl.when(i == 0)
        def _():
            pltpu.make_async_copy(oh.at[part(s)], out.at[:, cols(me)], l_o).start()

        @pl.when(i > 0)
        def _():
            remote(oh.at[part(s)], out.at[:, cols(me)], s_o, r_o, sc, score).start()

    loop(0, n, attend)

    drain(oh.at[part(0)], l_o)
    others = pl.ds(0, (n - 1) * HD)
    drain(out.at[:, others], r_o)
    drain(out.at[:, others], s_o)
    drain(out.at[:, others], s_q)
    drain(kv.at[0, pl.ds(0, (n - nt) * per)], s_kv)
    drain(kv.at[0, pl.ds(0, (n - nt) * per)], s_f)
    for core in range(nt):
        drain(kv.at[core, blocks(0)], s_s.at[core])


def halves_kernel(nc, lists, q, k, v, out, lv, ls, qh, kva, kvb, oh,
                  s_l, r_l, c_l, s_own, s_up, s_q, s_o, s_f, s_s, l_kv, r_kv, r_f, r_s, r_q, r_o):
    nt = 2
    n = nc * nt
    half = nc // 2
    row = half // 2
    rows = q.shape[0]
    per = rows // BLK
    kvs = (kva, kvb)
    c, t = lax.axis_index("seq"), lax.axis_index("tensor")
    me = c * nt + t
    sib = 1 - t
    hz, cx = c // half, lax.rem(c, half)
    base = hz * half
    tz = cx // row
    mine = lax.rem(cx, row) * nt + t

    def dev(chip, core):
        return {"seq": chip, "tensor": core}

    def blocks(index):
        return pl.ds(index * per, per)

    def cols(index, width):
        return pl.ds(pl.multiple_of(index * width, width), width)

    def remote(src, dst, send, recv, chip, core):
        return pltpu.make_async_remote_copy(
            src_ref=src, dst_ref=dst, send_sem=send, recv_sem=recv,
            device_id=dev(chip, core), device_id_type=MESH,
        )

    def drain(ref, sem):
        pltpu.make_async_copy(ref, ref, sem).wait()

    def loop(start, stop, step):
        def run(i, _):
            step(i)
            return 0
        lax.fori_loop(start, stop, run, 0)

    barrier = pltpu.get_barrier_semaphore()

    def greet(i):
        p = lax.rem(me + i, n)
        pl.semaphore_signal(barrier, inc=1, device_id=dev(p // nt, lax.rem(p, nt)), device_id_type=MESH)

    loop(1, n, greet)
    pl.semaphore_wait(barrier, n - 1)

    def send_kv(j, dc, sem):
        at = cols((lax.rem(dc, half)) * 2 + j, HD)
        for core, src in ((0, k), (1, v)):
            remote(src.at[:, :, at], kvs[j].at[core, blocks(me)], sem, r_kv.at[j, me], dc, core).start()

    def send_up(j):
        @pl.when(hz == 0)
        def _():
            loop(0, half, lambda i: send_kv(j, half + lax.rem(cx + i, half), s_up))

    def send_own(j):
        loop(1, half, lambda i: send_kv(j, base + lax.rem(cx + i, half), s_own))
        at = cols(cx * 2 + j, HD)
        for core, src in ((0, k), (1, v)):
            remote(src.at[:, :, at], kvs[j].at[core, blocks(me)], s_s.at[j, core], r_s.at[j, core], c, sib).start()
            pltpu.make_async_copy(src.at[:, :, at], kvs[j].at[core, blocks(me)], l_kv.at[j, core]).start()

    send_up(0)

    entry = lax.rem(me, 4)
    for far in range(2):
        dc = far * half + me // 4
        for core in range(nt):
            itself = (dc == c) & (t == core)

            @pl.when(itself)
            def _():
                pltpu.make_async_copy(lists, lv.at[entry], r_l.at[entry]).start()

            @pl.when(jnp.logical_not(itself))
            def _():
                remote(lists, lv.at[entry], s_l.at[far, core], r_l.at[entry], dc, core).start()

    send_own(0)

    def send_q(i):
        cl = lax.rem(cx + i, half)
        remote(q.at[:, cols(cl, 4 * HD)], qh.at[mine], s_q, r_q.at[mine], base + cl, tz).start()

    @pl.when(tz == t)
    def _():
        pltpu.make_async_copy(q.at[:, cols(cx, 4 * HD)], qh.at[mine], r_q.at[mine]).start()

    @pl.when(tz != t)
    def _():
        send_q(0)

    loop(1, half, send_q)
    send_up(1)
    send_own(1)

    def forward(j, chip):
        for core in range(nt):
            here = kvs[j].at[t, blocks(chip * nt + core)]
            drain(here, r_kv.at[j, chip * nt + core])
            remote(here, here, s_f.at[j], r_f.at[j], c, sib).start()

    def forward_own(j):
        loop(1, half, lambda i: forward(j, base + lax.rem(cx + half - i, half)))

    def settle(j):
        for core in range(nt):
            drain(kvs[j].at[core, blocks(0)], r_s.at[j, core])
            drain(kvs[j].at[core, blocks(0)], l_kv.at[j, core])

        @pl.when(hz == 0)
        def _():
            drain(kvs[j].at[0, pl.ds(0, (half - 1) * nt * per)], r_f.at[j])

        @pl.when(hz == 1)
        def _():
            drain(kvs[j].at[0, pl.ds(0, (nc - 1) * nt * per)], r_f.at[j])

    forward_own(0)

    @pl.when(hz == 1)
    def _():
        loop(0, half, lambda i: forward(0, lax.rem(cx + half - i, half)))

    for e in range(4):
        drain(lv.at[e], r_l.at[e])
    pltpu.make_async_copy(lv, ls, c_l).start()
    settle(0)
    pltpu.make_async_copy(lv, ls, c_l).wait()

    def attend(j, i):
        slot = lax.rem(mine + i, 4)
        sc, score = base + t * row + slot // nt, lax.rem(slot, nt)
        if j == 0:
            drain(qh.at[slot], r_q.at[slot])
        for inner in range(per):
            block = (sc * nt + score) * per + inner
            here = pl.ds(inner * BLK, BLK)
            for one in range(2):
                head = 2 * j + one
                listed = [ls[head, e, 0, block] for e in range(KSEL)]
                kcat = jnp.concatenate([kvs[j][0, e] for e in listed], axis=0)
                vcat = jnp.concatenate([kvs[j][1, e] for e in listed], axis=0)
                qblk = qh[slot, here, pl.ds(head * HD, HD)]
                oh[slot, j, here, pl.ds(one * HD, HD)] = attend_block(qblk, kcat, vcat, block)
        itself = (sc == c) & (score == t)
        goal = out.at[:, cols(cx * 2 + j, 2 * HD)]

        @pl.when(itself)
        def _():
            pltpu.make_async_copy(oh.at[slot, j], goal, r_o.at[cx, j]).start()

        @pl.when(jnp.logical_not(itself))
        def _():
            remote(oh.at[slot, j], goal, s_o, r_o.at[cx, j], sc, score).start()

    def first(i):
        @pl.when(i == 0)
        def _():
            forward_own(1)

        attend(0, i)

        @pl.when(hz == 1)
        def _():
            forward(1, lax.rem(cx + half - i, half))

    loop(0, 4, first)
    settle(1)
    loop(0, 4, lambda i: attend(1, i))

    for cl in range(half):
        for j in range(2):
            drain(out.at[:, pl.ds((cl * 2 + j) * 2 * HD, 2 * HD)], r_o.at[cl, j])

    @pl.when(tz == t)
    def _():
        drain(out.at[:, pl.ds(0, 3 * 4 * HD)], s_q)

    @pl.when(tz != t)
    def _():
        drain(out, s_q)

    @pl.when((base + t * row == c - lax.rem(cx, row)))
    def _():
        drain(out.at[:, pl.ds(0, 6 * 2 * HD)], s_o)

    @pl.when((base + t * row != c - lax.rem(cx, row)))
    def _():
        drain(out, s_o)

    drain(kva.at[0, pl.ds(0, (half - 1) * 4 * per)], s_own)

    @pl.when(hz == 0)
    def _():
        drain(kva.at[0], s_up)

    for j in range(2):
        @pl.when(hz == 0)
        def _():
            drain(kva.at[0, pl.ds(0, (half - 1) * nt * per)], s_f.at[j])

        @pl.when(hz == 1)
        def _():
            drain(kva.at[0, pl.ds(0, (nc - 1) * nt * per)], s_f.at[j])

        for core in range(nt):
            drain(kva.at[core, blocks(0)], s_s.at[j, core])

    for far in range(2):
        dc = far * half + me // 4
        for core in range(nt):
            @pl.when(jnp.logical_not((dc == c) & (t == core)))
            def _():
                drain(lv.at[0], s_l.at[far, core])


def halves(nc, queries, keys, values, block_lists):
    rows, width = queries.shape
    n = 2 * nc
    per = rows // BLK
    dma = pltpu.SemaphoreType.DMA
    hbm = pl.BlockSpec(memory_space=pl.ANY)
    entry = (KSEL, 1, block_lists.shape[1])
    kv = pltpu.VMEM((2, n * per, BLK, HD), jnp.bfloat16)
    return pl.pallas_call(
        functools.partial(halves_kernel, nc),
        out_shape=jax.ShapeDtypeStruct((rows, width), jnp.bfloat16),
        in_specs=[hbm, hbm, hbm, hbm],
        out_specs=hbm,
        scratch_shapes=[
            pltpu.VMEM((4, *entry), jnp.int32),
            pltpu.SMEM((4, *entry), jnp.int32),
            pltpu.VMEM((4, rows, 4 * HD), jnp.bfloat16),
            kv,
            kv,
            pltpu.VMEM((4, 2, rows, 2 * HD), jnp.bfloat16),
            dma((2, 2)), dma((4,)), dma, dma, dma, dma, dma, dma((2,)), dma((2, 2)), dma((2, 2)),
            dma((2, n)), dma((2,)), dma((2, 2)), dma((4,)), dma((nc // 2, 2)),
        ],
        compiler_params=pltpu.CompilerParams(
            collective_id=0, has_side_effects=True, vmem_limit_bytes=VMEM_MIB * 2**20
        ),
        cost_estimate=pl.CostEstimate(
            flops=4 * n * rows * KSEL * BLK * HD, bytes_accessed=8 * n * rows * HD, transcendentals=n * rows * KSEL * BLK
        ),
    )(block_lists.transpose(2, 0, 1), queries, keys.reshape(per, BLK, -1), values.reshape(per, BLK, -1))


def body(nc, nt, queries, keys, values, block_lists):
    rows, width = queries.shape
    n = nc * nt
    heads = width // HD
    kv_heads = keys.shape[1] // HD
    ratio = heads // kv_heads
    assert nt == 2 and heads == n and ratio % nt == 0 and rows % BLK == 0
    if nc == 8 and ratio == 2:
        return halves(nc, queries, keys, values, block_lists)
    mult = nc // 2 - 1 if nc >= 4 and nc & (nc - 1) == 0 else 1
    dma, shape = pltpu.SemaphoreType.DMA, jax.ShapeDtypeStruct
    hbm = pl.BlockSpec(memory_space=pl.ANY)
    return pl.pallas_call(
        functools.partial(kernel, nc, nt, ratio, mult),
        out_shape=shape((rows, width), jnp.bfloat16),
        in_specs=[pl.BlockSpec(memory_space=pltpu.SMEM), hbm, hbm, hbm],
        out_specs=hbm,
        scratch_shapes=[
            pltpu.VMEM((n * rows, HD), jnp.bfloat16),
            pltpu.VMEM((2, n * rows // BLK, BLK, HD), jnp.bfloat16),
            pltpu.VMEM((n * rows, HD), jnp.bfloat16),
            dma, dma, dma, dma, dma((nt,)), dma((nt,)), dma,
            dma((n,)), dma, dma((nt,)), dma((n,)), dma,
        ],
        compiler_params=pltpu.CompilerParams(
            collective_id=0, has_side_effects=True, vmem_limit_bytes=40 * 2**20
        ),
        cost_estimate=pl.CostEstimate(
            flops=4 * n * rows * KSEL * BLK * HD, bytes_accessed=8 * n * rows * HD, transcendentals=n * rows * KSEL * BLK
        ),
    )(
        block_lists.reshape(-1),
        queries,
        keys.reshape(rows // BLK, BLK, kv_heads * HD),
        values.reshape(rows // BLK, BLK, kv_heads * HD),
    )


def solution(mesh):
    placed = (
        P(("groups", "seq", "tensor"), None),
        P(("groups", "seq", "tensor"), None),
        P(("groups", "seq", "tensor"), None),
        P(("seq", "tensor"), None, None),
    )
    return jax.shard_map(
        functools.partial(body, mesh.shape["seq"], mesh.shape["tensor"]),
        mesh=mesh,
        in_specs=placed,
        out_specs=P(("groups", "seq", "tensor"), None),
        check_vma=False,
    )
```

```python
import functools

import jax
import jax.numpy as jnp
from jax import lax
from jax.experimental import pallas as pl
from jax.experimental.pallas import tpu as pltpu
from jax.sharding import PartitionSpec as P

HD = 128
BLK = 64
KSEL = 12
VMEM_MIB = 60
ORDER = (("own", 0), ("q", 0), ("up", 0), ("own", 1), ("q", 1), ("up", 1), ("own", 2), ("q", 2), ("up", 2))
MESH = pl.DeviceIdType.MESH
COEF = 1.4426950408889634 / (128.0**0.5)


def soften(raw, block):
    row = lax.broadcasted_iota(jnp.int32, raw.shape, 0)
    col = lax.broadcasted_iota(jnp.int32, raw.shape, 1)
    live = jnp.minimum(block + 1, KSEL) * BLK
    keep = ((col >= BLK) | (col <= row)) & (col < live)
    raw = jnp.where(keep, raw, jnp.float32(-1e30))
    top = jnp.max(raw, axis=1, keepdims=True)
    probs = jnp.exp2((raw - top) * jnp.float32(COEF))
    return probs.astype(jnp.bfloat16), jnp.sum(probs, axis=1, keepdims=True)


def attend_units(kv, units):
    raws = []
    for qblk, listed, _ in units:
        kcat = jnp.concatenate([kv[0, e] for e in listed], axis=0)
        raws.append(lax.dot_general(qblk, kcat, (((1,), (1,)), ((), ())), preferred_element_type=jnp.float32))
    soft = [soften(raw, block) for raw, (_, _, block) in zip(raws, units)]
    done = []
    for (probs, total), (_, listed, _) in zip(soft, units):
        vcat = jnp.concatenate([kv[1, e] for e in listed], axis=0)
        done.append((jnp.dot(probs, vcat, preferred_element_type=jnp.float32) / total).astype(jnp.bfloat16))
    return done


def kernel(nc, nt, ratio, mult, lists, q, k, v, out, qh, kv, oh,
           s_kv, s_q, s_o, s_f, s_s, l_kv, l_o, r_kv, r_f, r_s, r_q, r_o):
    n = nc * nt
    rows = q.shape[0]
    per = rows // BLK
    c, t = lax.axis_index("seq"), lax.axis_index("tensor")
    me = c * nt + t
    sib = 1 - t

    def dev(chip, core):
        return {"seq": chip, "tensor": core}

    def part(index):
        return pl.ds(pl.multiple_of(index * rows, rows), rows)

    def blocks(index):
        return pl.ds(index * per, per)

    def cols(head):
        return pl.ds(pl.multiple_of(head * HD, HD), HD)

    def remote(src, dst, send, recv, chip, core):
        return pltpu.make_async_remote_copy(
            src_ref=src, dst_ref=dst, send_sem=send, recv_sem=recv,
            device_id=dev(chip, core), device_id_type=MESH,
        )

    def drain(ref, sem):
        pltpu.make_async_copy(ref, ref, sem).wait()

    def loop(start, stop, step):
        def run(i, _):
            step(i)
            return 0
        lax.fori_loop(start, stop, run, 0)

    barrier = pltpu.get_barrier_semaphore()

    def greet(i):
        p = lax.rem(me + i, n)
        pl.semaphore_signal(barrier, inc=1, device_id=dev(p // nt, lax.rem(p, nt)), device_id_type=MESH)

    loop(1, n, greet)
    pl.semaphore_wait(barrier, n - 1)

    def send_kv(j):
        dc = lax.rem(c + j * mult, nc)
        head = cols((dc * nt) // ratio)
        for core, src in ((0, k), (1, v)):
            remote(src.at[:, :, head], kv.at[core, blocks(me)], s_kv, r_kv.at[me], dc, core).start()

    loop(1, nc, send_kv)
    head = cols(me // ratio)
    local = []
    for core, src in ((0, k), (1, v)):
        remote(src.at[:, :, head], kv.at[core, blocks(me)], s_s.at[core], r_s.at[core], c, sib).start()
        local.append(pltpu.make_async_copy(src.at[:, :, head], kv.at[core, blocks(me)], l_kv.at[core]))
        local[-1].start()

    pltpu.make_async_copy(q.at[:, cols(me)], qh.at[part(me)], r_q.at[me]).start()
    remote(q.at[:, cols(c * nt + sib)], qh.at[part(me)], s_q, r_q.at[me], c, sib).start()

    def send_q(j):
        dc = lax.rem(c + j * mult, nc)
        for core in range(nt):
            remote(q.at[:, cols(dc * nt + core)], qh.at[part(me)], s_q, r_q.at[me], dc, core).start()

    loop(1, nc, send_q)

    def forward(j):
        sc = lax.rem(c + (nc - j) * mult, nc)
        for core in range(nt):
            s = sc * nt + core
            drain(kv.at[t, blocks(s)], r_kv.at[s])
            remote(kv.at[t, blocks(s)], kv.at[t, blocks(s)], s_f, r_f, c, sib).start()

    loop(1, nc, forward)
    for core in range(nt):
        local[core].wait()
        drain(kv.at[core, blocks(0)], r_s.at[core])
    drain(kv.at[0, pl.ds(0, (n - nt) * per)], r_f)

    def attend(i):
        j = i // nt
        sc = lax.rem(c + (nc - j) * mult, nc)
        score = lax.rem(t + i, nt)
        s = sc * nt + score
        drain(qh.at[part(s)], r_q.at[s])
        units, places = [], []
        for inner in range(per):
            block = s * per + inner
            places.append(pl.ds(pl.multiple_of(block * BLK, BLK), BLK))
            units.append((qh[places[-1], :], [lists[block * KSEL + e] for e in range(KSEL)], block))
        for here, made in zip(places, attend_units(kv, units)):
            oh[here, :] = made

        @pl.when(i == 0)
        def _():
            pltpu.make_async_copy(oh.at[part(s)], out.at[:, cols(me)], l_o).start()

        @pl.when(i > 0)
        def _():
            remote(oh.at[part(s)], out.at[:, cols(me)], s_o, r_o, sc, score).start()

    loop(0, n, attend)

    drain(oh.at[part(0)], l_o)
    others = pl.ds(0, (n - 1) * HD)
    drain(out.at[:, others], r_o)
    drain(out.at[:, others], s_o)
    drain(out.at[:, others], s_q)
    drain(kv.at[0, pl.ds(0, (n - nt) * per)], s_kv)
    drain(kv.at[0, pl.ds(0, (n - nt) * per)], s_f)
    for core in range(nt):
        drain(kv.at[core, blocks(0)], s_s.at[core])


def halves_kernel(nc, lists, q, k, v, out, lv, ls, qh, kv0, kv1, kv2, oh,
                  s_l, r_l, c_l, s_own, s_up, s_q, s_o, s_f, s_s, l_kv, r_kv, r_f, r_s, r_q, r_o):
    nt = 2
    n = nc * nt
    half = nc // 2
    row = half // 2
    rows = q.shape[0]
    per = rows // BLK
    wide = 2 * HD
    kvs = (kv0, kv1, kv2)
    last = len(kvs) - 1
    c, t = lax.axis_index("seq"), lax.axis_index("tensor")
    me = c * nt + t
    sib = 1 - t
    hz, cx = c // half, lax.rem(c, half)
    base = hz * half
    tz = cx // row
    mine = lax.rem(cx, row) * nt + t
    own_row = tz == t

    def dev(chip, core):
        return {"seq": chip, "tensor": core}

    def key_head(p, cl):
        return jnp.where(cl < row, 3 * cl + p, 3 * row + cl - row)

    def blocks(index):
        return pl.ds(index * per, per)

    def cols(index, width):
        return pl.ds(pl.multiple_of(index * width, width), width)

    def remote(src, dst, send, recv, chip, core):
        return pltpu.make_async_remote_copy(
            src_ref=src, dst_ref=dst, send_sem=send, recv_sem=recv,
            device_id=dev(chip, core), device_id_type=MESH,
        )

    def drain(ref, sem):
        pltpu.make_async_copy(ref, ref, sem).wait()

    def loop(start, stop, step):
        def run(i, _):
            step(i)
            return 0
        lax.fori_loop(start, stop, run, 0)

    def where(*cases):
        for condition, act in cases:
            pl.when(condition)(act)

    barrier = pltpu.get_barrier_semaphore()

    def greet(i):
        p = lax.rem(me + i, n)
        pl.semaphore_signal(barrier, inc=1, device_id=dev(p // nt, lax.rem(p, nt)), device_id_type=MESH)

    loop(1, n, greet)
    pl.semaphore_wait(barrier, n - 1)

    def send_kv(p, chip, sem):
        at = cols(key_head(p, lax.rem(chip, half)), HD)
        for core, src in ((0, k), (1, v)):
            remote(src.at[:, :, at], kvs[p].at[core, blocks(me)], sem, r_kv.at[p, me], chip, core).start()

    def dests(p):
        return half if p == last else row

    def send_up(p):
        where((hz == 0, lambda: loop(0, dests(p), lambda i: send_kv(p, half + lax.rem(cx + i, dests(p)), s_up))))

    def send_own(p):
        def one(i):
            cl = lax.rem(cx + i, dests(p))
            where((cl != cx, lambda: send_kv(p, base + cl, s_own)))

        loop(0, dests(p), one)

        def within():
            at = cols(key_head(p, cx), HD)
            for core, src in ((0, k), (1, v)):
                goal = kvs[p].at[core, blocks(me)]
                remote(src.at[:, :, at], goal, s_s.at[p, core], r_s.at[p, core], c, sib).start()
                pltpu.make_async_copy(src.at[:, :, at], goal, l_kv.at[p, core]).start()

        where((cx < dests(p), within))

    def send_q(p):
        def one(i):
            cl = lax.rem(cx + i, dests(p))
            src, goal = q.at[:, cols(key_head(p, cl), wide)], qh.at[mine, p]
            itself = (cl == cx) & own_row
            where(
                (itself, lambda: pltpu.make_async_copy(src, goal, r_q.at[mine, p]).start()),
                (jnp.logical_not(itself), lambda: remote(src, goal, s_q, r_q.at[mine, p], base + cl, tz).start()),
            )

        loop(0, dests(p), one)

    group = me // 2
    early = group < 3 * row
    list_chip = jnp.where(early, group // 3, group - 2 * row)
    entry = jnp.where(early, lax.rem(group, 3), last) * 2 + lax.rem(me, 2)

    def each_list(act_self, act_other):
        for far in range(2):
            for core in range(nt):
                chip = far * half + list_chip
                itself = (chip == c) & (t == core)
                where(
                    (itself, act_self),
                    (jnp.logical_not(itself), functools.partial(act_other, far, core, chip)),
                )

    def send_lists():
        each_list(
            lambda: pltpu.make_async_copy(lists, lv.at[entry], r_l.at[entry]).start(),
            lambda far, core, chip: remote(lists, lv.at[entry], s_l.at[far, core], r_l.at[entry], chip, core).start(),
        )

    send_lists()
    for name, p in ORDER:
        {"up": send_up, "own": send_own, "q": send_q}[name](p)

    def forward(p, chip):
        for core in range(nt):
            here = kvs[p].at[t, blocks(chip * nt + core)]
            drain(here, r_kv.at[p, chip * nt + core])
            remote(here, here, s_f.at[p], r_f.at[p], c, sib).start()

    def forward_own(p):
        loop(1, half, lambda i: forward(p, base + lax.rem(cx + half - i, half)))

    def forward_low(p, i):
        where((hz == 1, lambda: forward(p, lax.rem(cx + half - i, half))))

    def forward_all(p):
        forward_own(p)
        loop(0, half, functools.partial(forward_low, p))

    def drain_forwards(p, sem):
        where(
            (hz == 0, lambda: drain(kvs[p].at[0, pl.ds(0, (half - 1) * nt * per)], sem)),
            (hz == 1, lambda: drain(kvs[p].at[0, pl.ds(0, (nc - 1) * nt * per)], sem)),
        )

    def settle(p):
        for core in range(nt):
            drain(kvs[p].at[core, blocks(0)], r_s.at[p, core])
            drain(kvs[p].at[core, blocks(0)], l_kv.at[p, core])
        drain_forwards(p, r_f.at[p])

    def take_lists(start, stop, sem):
        for e in range(start, stop):
            drain(lv.at[e], r_l.at[e])
        some = pl.ds(start, stop - start)
        moved = pltpu.make_async_copy(lv.at[some], ls.at[some], sem)
        moved.start()
        moved.wait()

    def attend(p, i):
        slot = lax.rem(mine + i, 4)
        sc, score = base + t * row + slot // nt, lax.rem(slot, nt)
        drain(qh.at[slot, p], r_q.at[slot, p])
        units, places = [], []
        for inner in range(per):
            block = (sc * nt + score) * per + inner
            for one in range(2):
                listed = [ls[2 * p + one, e, 0, block] for e in range(KSEL)]
                here = pl.ds(inner * BLK, BLK), pl.ds(one * HD, HD)
                places.append(here)
                units.append((qh[slot, p, here[0], here[1]], listed, block))
        for here, made in zip(places, attend_units(kvs[p], units)):
            oh[slot, p, here[0], here[1]] = made
        itself = (sc == c) & (score == t)
        head = key_head(p, cx)
        src, goal = oh.at[slot, p], out.at[:, cols(head, wide)]
        where(
            (itself, lambda: pltpu.make_async_copy(src, goal, r_o.at[head]).start()),
            (jnp.logical_not(itself), lambda: remote(src, goal, s_o, r_o.at[head], sc, score).start()),
        )

    def attend_and_forward(p, i):
        where((i == 0, lambda: forward_own(p + 1)))
        attend(p, i)
        forward_low(p + 1, i)

    def row_zero():
        forward_all(0)
        take_lists(0, 2 * last, c_l.at[0])
        for p in range(last):
            settle(p)
            loop(0, 4, functools.partial(attend_and_forward, p))

    where((tz == 0, row_zero), (tz == 1, lambda: forward_all(last)))
    take_lists(2 * last, 2 * last + 2, c_l.at[1])
    settle(last)
    loop(0, 4, functools.partial(attend, last))

    for head in range(8):
        drain(out.at[:, pl.ds(head * wide, wide)], r_o.at[head])

    def drain_q(count):
        drain(out.at[:, pl.ds(0, count * wide)], s_q)

    where(
        (jnp.logical_not(own_row), lambda: drain_q(8)),
        (own_row & (tz == 0), lambda: drain_q(5)),
        (own_row & (tz == 1), lambda: drain_q(7)),
        (jnp.logical_not(own_row) & (tz == 0), lambda: drain(oh, s_o)),
        (jnp.logical_not(own_row) & (tz == 1), lambda: drain(oh.at[:, 0], s_o)),
        (own_row & (tz == 0), lambda: drain(oh.at[pl.ds(0, 3)], s_o)),
        (own_row & (tz == 1), lambda: drain(oh.at[pl.ds(0, 3), 0], s_o)),
        (tz == 0, lambda: drain(kv0.at[0, pl.ds(0, 10 * per)], s_own)),
        (tz == 1, lambda: drain(kv0.at[0, pl.ds(0, 14 * per)], s_own)),
        (hz == 0, lambda: drain(kv0.at[0], s_up)),
    )

    def drain_phase(p):
        drain_forwards(p, s_f.at[p])
        for core in range(nt):
            drain(kvs[p].at[core, blocks(0)], s_s.at[p, core])

    where((tz == 0, lambda: [drain_phase(p) for p in range(last)] and None))
    drain_phase(last)
    each_list(lambda: None, lambda far, core, chip: drain(lv.at[0], s_l.at[far, core]))


def halves(nc, queries, keys, values, block_lists):
    rows, width = queries.shape
    n = 2 * nc
    per = rows // BLK
    dma = pltpu.SemaphoreType.DMA
    hbm = pl.BlockSpec(memory_space=pl.ANY)
    entry = (KSEL, 1, block_lists.shape[1])
    kv = pltpu.VMEM((2, n * per, BLK, HD), jnp.bfloat16)
    return pl.pallas_call(
        functools.partial(halves_kernel, nc),
        out_shape=jax.ShapeDtypeStruct((rows, width), jnp.bfloat16),
        in_specs=[hbm, hbm, hbm, hbm],
        out_specs=hbm,
        scratch_shapes=[
            pltpu.VMEM((6, *entry), jnp.int32),
            pltpu.SMEM((6, *entry), jnp.int32),
            pltpu.VMEM((4, 3, rows, 2 * HD), jnp.bfloat16),
            kv,
            kv,
            kv,
            pltpu.VMEM((4, 3, rows, 2 * HD), jnp.bfloat16),
            dma((2, 2)), dma((6,)), dma((2,)), dma, dma, dma, dma, dma((3,)), dma((3, 2)), dma((3, 2)),
            dma((3, n)), dma((3,)), dma((3, 2)), dma((4, 3)), dma((8,)),
        ],
        compiler_params=pltpu.CompilerParams(
            collective_id=0, has_side_effects=True, vmem_limit_bytes=VMEM_MIB * 2**20
        ),
        cost_estimate=pl.CostEstimate(
            flops=4 * n * rows * KSEL * BLK * HD, bytes_accessed=8 * n * rows * HD, transcendentals=n * rows * KSEL * BLK
        ),
    )(block_lists.transpose(2, 0, 1), queries, keys.reshape(per, BLK, -1), values.reshape(per, BLK, -1))


def body(nc, nt, queries, keys, values, block_lists):
    rows, width = queries.shape
    n = nc * nt
    heads = width // HD
    kv_heads = keys.shape[1] // HD
    ratio = heads // kv_heads
    assert nt == 2 and heads == n and ratio % nt == 0 and rows % BLK == 0
    if nc == 8 and ratio == 2:
        return halves(nc, queries, keys, values, block_lists)
    mult = nc // 2 - 1 if nc >= 4 and nc & (nc - 1) == 0 else 1
    dma, shape = pltpu.SemaphoreType.DMA, jax.ShapeDtypeStruct
    hbm = pl.BlockSpec(memory_space=pl.ANY)
    return pl.pallas_call(
        functools.partial(kernel, nc, nt, ratio, mult),
        out_shape=shape((rows, width), jnp.bfloat16),
        in_specs=[pl.BlockSpec(memory_space=pltpu.SMEM), hbm, hbm, hbm],
        out_specs=hbm,
        scratch_shapes=[
            pltpu.VMEM((n * rows, HD), jnp.bfloat16),
            pltpu.VMEM((2, n * rows // BLK, BLK, HD), jnp.bfloat16),
            pltpu.VMEM((n * rows, HD), jnp.bfloat16),
            dma, dma, dma, dma, dma((nt,)), dma((nt,)), dma,
            dma((n,)), dma, dma((nt,)), dma((n,)), dma,
        ],
        compiler_params=pltpu.CompilerParams(
            collective_id=0, has_side_effects=True, vmem_limit_bytes=40 * 2**20
        ),
        cost_estimate=pl.CostEstimate(
            flops=4 * n * rows * KSEL * BLK * HD, bytes_accessed=8 * n * rows * HD, transcendentals=n * rows * KSEL * BLK
        ),
    )(
        block_lists.reshape(-1),
        queries,
        keys.reshape(rows // BLK, BLK, kv_heads * HD),
        values.reshape(rows // BLK, BLK, kv_heads * HD),
    )


def solution(mesh):
    placed = (
        P(("groups", "seq", "tensor"), None),
        P(("groups", "seq", "tensor"), None),
        P(("groups", "seq", "tensor"), None),
        P(("seq", "tensor"), None, None),
    )
    return jax.shard_map(
        functools.partial(body, mesh.shape["seq"], mesh.shape["tensor"]),
        mesh=mesh,
        in_specs=placed,
        out_specs=P(("groups", "seq", "tensor"), None),
        check_vma=False,
    )
```

```python
import functools

import jax
import jax.numpy as jnp
from jax import lax
from jax.experimental import pallas as pl
from jax.experimental.pallas import tpu as pltpu
from jax.sharding import PartitionSpec as P

HD = 128
BLK = 64
KSEL = 12
VMEM_MIB = 60
MESH = pl.DeviceIdType.MESH
COEF = 1.4426950408889634 / (128.0**0.5)


def soften(raw, block):
    row = lax.broadcasted_iota(jnp.int32, raw.shape, 0)
    col = lax.broadcasted_iota(jnp.int32, raw.shape, 1)
    live = jnp.minimum(block + 1, KSEL) * BLK
    keep = ((col >= BLK) | (col <= row)) & (col < live)
    raw = jnp.where(keep, raw, jnp.float32(-1e30))
    top = jnp.max(raw, axis=1, keepdims=True)
    probs = jnp.exp2((raw - top) * jnp.float32(COEF))
    return probs.astype(jnp.bfloat16), jnp.sum(probs, axis=1, keepdims=True)


def attend_units(kv, units):
    raws = []
    for qblk, listed, _ in units:
        kcat = jnp.concatenate([kv[0, e] for e in listed], axis=0)
        raws.append(lax.dot_general(qblk, kcat, (((1,), (1,)), ((), ())), preferred_element_type=jnp.float32))
    soft = [soften(raw, block) for raw, (_, _, block) in zip(raws, units)]
    done = []
    for (probs, total), (_, listed, _) in zip(soft, units):
        vcat = jnp.concatenate([kv[1, e] for e in listed], axis=0)
        done.append((jnp.dot(probs, vcat, preferred_element_type=jnp.float32) / total).astype(jnp.bfloat16))
    return done


def kernel(nc, nt, ratio, mult, lists, q, k, v, out, qh, kv, oh,
           s_kv, s_q, s_o, s_f, s_s, l_kv, l_o, r_kv, r_f, r_s, r_q, r_o):
    n = nc * nt
    rows = q.shape[0]
    per = rows // BLK
    c, t = lax.axis_index("seq"), lax.axis_index("tensor")
    me = c * nt + t
    sib = 1 - t

    def dev(chip, core):
        return {"seq": chip, "tensor": core}

    def part(index):
        return pl.ds(pl.multiple_of(index * rows, rows), rows)

    def blocks(index):
        return pl.ds(index * per, per)

    def cols(head):
        return pl.ds(pl.multiple_of(head * HD, HD), HD)

    def remote(src, dst, send, recv, chip, core):
        return pltpu.make_async_remote_copy(
            src_ref=src, dst_ref=dst, send_sem=send, recv_sem=recv,
            device_id=dev(chip, core), device_id_type=MESH,
        )

    def drain(ref, sem):
        pltpu.make_async_copy(ref, ref, sem).wait()

    def loop(start, stop, step):
        def run(i, _):
            step(i)
            return 0
        lax.fori_loop(start, stop, run, 0)

    barrier = pltpu.get_barrier_semaphore()

    def greet(i):
        p = lax.rem(me + i, n)
        pl.semaphore_signal(barrier, inc=1, device_id=dev(p // nt, lax.rem(p, nt)), device_id_type=MESH)

    loop(1, n, greet)
    pl.semaphore_wait(barrier, n - 1)

    def send_kv(j):
        dc = lax.rem(c + j * mult, nc)
        head = cols((dc * nt) // ratio)
        for core, src in ((0, k), (1, v)):
            remote(src.at[:, :, head], kv.at[core, blocks(me)], s_kv, r_kv.at[me], dc, core).start()

    loop(1, nc, send_kv)
    head = cols(me // ratio)
    local = []
    for core, src in ((0, k), (1, v)):
        remote(src.at[:, :, head], kv.at[core, blocks(me)], s_s.at[core], r_s.at[core], c, sib).start()
        local.append(pltpu.make_async_copy(src.at[:, :, head], kv.at[core, blocks(me)], l_kv.at[core]))
        local[-1].start()

    pltpu.make_async_copy(q.at[:, cols(me)], qh.at[part(me)], r_q.at[me]).start()
    remote(q.at[:, cols(c * nt + sib)], qh.at[part(me)], s_q, r_q.at[me], c, sib).start()

    def send_q(j):
        dc = lax.rem(c + j * mult, nc)
        for core in range(nt):
            remote(q.at[:, cols(dc * nt + core)], qh.at[part(me)], s_q, r_q.at[me], dc, core).start()

    loop(1, nc, send_q)

    def forward(j):
        sc = lax.rem(c + (nc - j) * mult, nc)
        for core in range(nt):
            s = sc * nt + core
            drain(kv.at[t, blocks(s)], r_kv.at[s])
            remote(kv.at[t, blocks(s)], kv.at[t, blocks(s)], s_f, r_f, c, sib).start()

    loop(1, nc, forward)
    for core in range(nt):
        local[core].wait()
        drain(kv.at[core, blocks(0)], r_s.at[core])
    drain(kv.at[0, pl.ds(0, (n - nt) * per)], r_f)

    def attend(i):
        j = i // nt
        sc = lax.rem(c + (nc - j) * mult, nc)
        score = lax.rem(t + i, nt)
        s = sc * nt + score
        drain(qh.at[part(s)], r_q.at[s])
        units, places = [], []
        for inner in range(per):
            block = s * per + inner
            places.append(pl.ds(pl.multiple_of(block * BLK, BLK), BLK))
            units.append((qh[places[-1], :], [lists[block * KSEL + e] for e in range(KSEL)], block))
        for here, made in zip(places, attend_units(kv, units)):
            oh[here, :] = made

        @pl.when(i == 0)
        def _():
            pltpu.make_async_copy(oh.at[part(s)], out.at[:, cols(me)], l_o).start()

        @pl.when(i > 0)
        def _():
            remote(oh.at[part(s)], out.at[:, cols(me)], s_o, r_o, sc, score).start()

    loop(0, n, attend)

    drain(oh.at[part(0)], l_o)
    others = pl.ds(0, (n - 1) * HD)
    drain(out.at[:, others], r_o)
    drain(out.at[:, others], s_o)
    drain(out.at[:, others], s_q)
    drain(kv.at[0, pl.ds(0, (n - nt) * per)], s_kv)
    drain(kv.at[0, pl.ds(0, (n - nt) * per)], s_f)
    for core in range(nt):
        drain(kv.at[core, blocks(0)], s_s.at[core])


def halves_kernel(nc, lists, q, k, v, out, lv, ls, qh, kva, kvb, oh,
                  s_l, r_l, c_l, s_own, s_up, s_q, s_o, s_f, s_s, l_kv, r_kv, r_f, r_s, r_q, r_o):
    nt = 2
    n = nc * nt
    half = nc // 2
    row = half // 2
    rows = q.shape[0]
    per = rows // BLK
    kvs = (kva, kvb)
    c, t = lax.axis_index("seq"), lax.axis_index("tensor")
    me = c * nt + t
    sib = 1 - t
    hz, cx = c // half, lax.rem(c, half)
    base = hz * half
    tz = cx // row
    mine = lax.rem(cx, row) * nt + t

    def dev(chip, core):
        return {"seq": chip, "tensor": core}

    def blocks(index):
        return pl.ds(index * per, per)

    def cols(index, width):
        return pl.ds(pl.multiple_of(index * width, width), width)

    def remote(src, dst, send, recv, chip, core):
        return pltpu.make_async_remote_copy(
            src_ref=src, dst_ref=dst, send_sem=send, recv_sem=recv,
            device_id=dev(chip, core), device_id_type=MESH,
        )

    def drain(ref, sem):
        pltpu.make_async_copy(ref, ref, sem).wait()

    def loop(start, stop, step):
        def run(i, _):
            step(i)
            return 0
        lax.fori_loop(start, stop, run, 0)

    barrier = pltpu.get_barrier_semaphore()

    def greet(i):
        p = lax.rem(me + i, n)
        pl.semaphore_signal(barrier, inc=1, device_id=dev(p // nt, lax.rem(p, nt)), device_id_type=MESH)

    loop(1, n, greet)
    pl.semaphore_wait(barrier, n - 1)

    def send_kv(j, dc, sem):
        at = cols((lax.rem(dc, half)) * 2 + j, HD)
        for core, src in ((0, k), (1, v)):
            remote(src.at[:, :, at], kvs[j].at[core, blocks(me)], sem, r_kv.at[j, me], dc, core).start()

    def send_up(j):
        @pl.when(hz == 0)
        def _():
            loop(0, half, lambda i: send_kv(j, half + lax.rem(cx + i, half), s_up))

    def send_own(j):
        loop(1, half, lambda i: send_kv(j, base + lax.rem(cx + i, half), s_own))
        at = cols(cx * 2 + j, HD)
        for core, src in ((0, k), (1, v)):
            remote(src.at[:, :, at], kvs[j].at[core, blocks(me)], s_s.at[j, core], r_s.at[j, core], c, sib).start()
            pltpu.make_async_copy(src.at[:, :, at], kvs[j].at[core, blocks(me)], l_kv.at[j, core]).start()

    entry = lax.rem(me, 4)
    for far in range(2):
        dc = far * half + me // 4
        for core in range(nt):
            itself = (dc == c) & (t == core)

            @pl.when(itself)
            def _():
                pltpu.make_async_copy(lists, lv.at[entry], r_l.at[entry]).start()

            @pl.when(jnp.logical_not(itself))
            def _():
                remote(lists, lv.at[entry], s_l.at[far, core], r_l.at[entry], dc, core).start()

    send_own(0)

    def send_q(i):
        cl = lax.rem(cx + i, half)
        remote(q.at[:, cols(cl, 4 * HD)], qh.at[mine], s_q, r_q.at[mine], base + cl, tz).start()

    @pl.when(tz == t)
    def _():
        pltpu.make_async_copy(q.at[:, cols(cx, 4 * HD)], qh.at[mine], r_q.at[mine]).start()

    @pl.when(tz != t)
    def _():
        send_q(0)

    loop(1, half, send_q)
    send_own(1)
    send_up(0)
    send_up(1)

    def forward(j, chip):
        for core in range(nt):
            here = kvs[j].at[t, blocks(chip * nt + core)]
            drain(here, r_kv.at[j, chip * nt + core])
            remote(here, here, s_f.at[j], r_f.at[j], c, sib).start()

    def forward_own(j):
        loop(1, half, lambda i: forward(j, base + lax.rem(cx + half - i, half)))

    def settle(j):
        for core in range(nt):
            drain(kvs[j].at[core, blocks(0)], r_s.at[j, core])
            drain(kvs[j].at[core, blocks(0)], l_kv.at[j, core])

        @pl.when(hz == 0)
        def _():
            drain(kvs[j].at[0, pl.ds(0, (half - 1) * nt * per)], r_f.at[j])

        @pl.when(hz == 1)
        def _():
            drain(kvs[j].at[0, pl.ds(0, (nc - 1) * nt * per)], r_f.at[j])

    forward_own(0)

    @pl.when(hz == 1)
    def _():
        loop(0, half, lambda i: forward(0, lax.rem(cx + half - i, half)))

    for e in range(4):
        drain(lv.at[e], r_l.at[e])
    pltpu.make_async_copy(lv, ls, c_l).start()
    settle(0)
    pltpu.make_async_copy(lv, ls, c_l).wait()

    def attend(j, i):
        slot = lax.rem(mine + i, 4)
        sc, score = base + t * row + slot // nt, lax.rem(slot, nt)
        if j == 0:
            drain(qh.at[slot], r_q.at[slot])
        units, places = [], []
        for inner in range(per):
            block = (sc * nt + score) * per + inner
            for one in range(2):
                head = 2 * j + one
                listed = [ls[head, e, 0, block] for e in range(KSEL)]
                here = pl.ds(inner * BLK, BLK)
                places.append((here, pl.ds(one * HD, HD)))
                units.append((qh[slot, here, pl.ds(head * HD, HD)], listed, block))
        for here, made in zip(places, attend_units(kvs[j], units)):
            oh[slot, j, here[0], here[1]] = made
        itself = (sc == c) & (score == t)
        goal = out.at[:, cols(cx * 2 + j, 2 * HD)]

        @pl.when(itself)
        def _():
            pltpu.make_async_copy(oh.at[slot, j], goal, r_o.at[cx, j]).start()

        @pl.when(jnp.logical_not(itself))
        def _():
            remote(oh.at[slot, j], goal, s_o, r_o.at[cx, j], sc, score).start()

    def first(i):
        @pl.when(i == 0)
        def _():
            forward_own(1)

        attend(0, i)

        @pl.when(hz == 1)
        def _():
            forward(1, lax.rem(cx + half - i, half))

    loop(0, 4, first)
    settle(1)
    loop(0, 4, lambda i: attend(1, i))

    for cl in range(half):
        for j in range(2):
            drain(out.at[:, pl.ds((cl * 2 + j) * 2 * HD, 2 * HD)], r_o.at[cl, j])

    @pl.when(tz == t)
    def _():
        drain(out.at[:, pl.ds(0, 3 * 4 * HD)], s_q)

    @pl.when(tz != t)
    def _():
        drain(out, s_q)

    @pl.when((base + t * row == c - lax.rem(cx, row)))
    def _():
        drain(out.at[:, pl.ds(0, 6 * 2 * HD)], s_o)

    @pl.when((base + t * row != c - lax.rem(cx, row)))
    def _():
        drain(out, s_o)

    drain(kva.at[0, pl.ds(0, (half - 1) * 4 * per)], s_own)

    @pl.when(hz == 0)
    def _():
        drain(kva.at[0], s_up)

    for j in range(2):
        @pl.when(hz == 0)
        def _():
            drain(kva.at[0, pl.ds(0, (half - 1) * nt * per)], s_f.at[j])

        @pl.when(hz == 1)
        def _():
            drain(kva.at[0, pl.ds(0, (nc - 1) * nt * per)], s_f.at[j])

        for core in range(nt):
            drain(kva.at[core, blocks(0)], s_s.at[j, core])

    for far in range(2):
        dc = far * half + me // 4
        for core in range(nt):
            @pl.when(jnp.logical_not((dc == c) & (t == core)))
            def _():
                drain(lv.at[0], s_l.at[far, core])


def halves(nc, queries, keys, values, block_lists):
    rows, width = queries.shape
    n = 2 * nc
    per = rows // BLK
    dma = pltpu.SemaphoreType.DMA
    hbm = pl.BlockSpec(memory_space=pl.ANY)
    entry = (KSEL, 1, block_lists.shape[1])
    kv = pltpu.VMEM((2, n * per, BLK, HD), jnp.bfloat16)
    return pl.pallas_call(
        functools.partial(halves_kernel, nc),
        out_shape=jax.ShapeDtypeStruct((rows, width), jnp.bfloat16),
        in_specs=[hbm, hbm, hbm, hbm],
        out_specs=hbm,
        scratch_shapes=[
            pltpu.VMEM((4, *entry), jnp.int32),
            pltpu.SMEM((4, *entry), jnp.int32),
            pltpu.VMEM((4, rows, 4 * HD), jnp.bfloat16),
            kv,
            kv,
            pltpu.VMEM((4, 2, rows, 2 * HD), jnp.bfloat16),
            dma((2, 2)), dma((4,)), dma, dma, dma, dma, dma, dma((2,)), dma((2, 2)), dma((2, 2)),
            dma((2, n)), dma((2,)), dma((2, 2)), dma((4,)), dma((nc // 2, 2)),
        ],
        compiler_params=pltpu.CompilerParams(
            collective_id=0, has_side_effects=True, vmem_limit_bytes=VMEM_MIB * 2**20
        ),
        cost_estimate=pl.CostEstimate(
            flops=4 * n * rows * KSEL * BLK * HD, bytes_accessed=8 * n * rows * HD, transcendentals=n * rows * KSEL * BLK
        ),
    )(block_lists.transpose(2, 0, 1), queries, keys.reshape(per, BLK, -1), values.reshape(per, BLK, -1))


def body(nc, nt, queries, keys, values, block_lists):
    rows, width = queries.shape
    n = nc * nt
    heads = width // HD
    kv_heads = keys.shape[1] // HD
    ratio = heads // kv_heads
    assert nt == 2 and heads == n and ratio % nt == 0 and rows % BLK == 0
    if nc == 8 and ratio == 2:
        return halves(nc, queries, keys, values, block_lists)
    mult = nc // 2 - 1 if nc >= 4 and nc & (nc - 1) == 0 else 1
    dma, shape = pltpu.SemaphoreType.DMA, jax.ShapeDtypeStruct
    hbm = pl.BlockSpec(memory_space=pl.ANY)
    return pl.pallas_call(
        functools.partial(kernel, nc, nt, ratio, mult),
        out_shape=shape((rows, width), jnp.bfloat16),
        in_specs=[pl.BlockSpec(memory_space=pltpu.SMEM), hbm, hbm, hbm],
        out_specs=hbm,
        scratch_shapes=[
            pltpu.VMEM((n * rows, HD), jnp.bfloat16),
            pltpu.VMEM((2, n * rows // BLK, BLK, HD), jnp.bfloat16),
            pltpu.VMEM((n * rows, HD), jnp.bfloat16),
            dma, dma, dma, dma, dma((nt,)), dma((nt,)), dma,
            dma((n,)), dma, dma((nt,)), dma((n,)), dma,
        ],
        compiler_params=pltpu.CompilerParams(
            collective_id=0, has_side_effects=True, vmem_limit_bytes=40 * 2**20
        ),
        cost_estimate=pl.CostEstimate(
            flops=4 * n * rows * KSEL * BLK * HD, bytes_accessed=8 * n * rows * HD, transcendentals=n * rows * KSEL * BLK
        ),
    )(
        block_lists.reshape(-1),
        queries,
        keys.reshape(rows // BLK, BLK, kv_heads * HD),
        values.reshape(rows // BLK, BLK, kv_heads * HD),
    )


def solution(mesh):
    placed = (
        P(("groups", "seq", "tensor"), None),
        P(("groups", "seq", "tensor"), None),
        P(("groups", "seq", "tensor"), None),
        P(("seq", "tensor"), None, None),
    )
    return jax.shard_map(
        functools.partial(body, mesh.shape["seq"], mesh.shape["tensor"]),
        mesh=mesh,
        in_specs=placed,
        out_specs=P(("groups", "seq", "tensor"), None),
        check_vma=False,
    )
```

```python
import functools

import jax
import jax.numpy as jnp
from jax import lax
from jax.experimental import pallas as pl
from jax.experimental.pallas import tpu as pltpu
from jax.sharding import PartitionSpec as P

HD = 128
BLK = 64
KSEL = 12
VMEM_MIB = 60
MESH = pl.DeviceIdType.MESH
COEF = 1.4426950408889634 / (128.0**0.5)


def soften(raw, block):
    row = lax.broadcasted_iota(jnp.int32, raw.shape, 0)
    col = lax.broadcasted_iota(jnp.int32, raw.shape, 1)
    live = jnp.minimum(block + 1, KSEL) * BLK
    keep = ((col >= BLK) | (col <= row)) & (col < live)
    raw = jnp.where(keep, raw, jnp.float32(-1e30))
    top = jnp.max(raw, axis=1, keepdims=True)
    probs = jnp.exp2((raw - top) * jnp.float32(COEF))
    return probs.astype(jnp.bfloat16), jnp.sum(probs, axis=1, keepdims=True)


def attend_units(kv, units):
    raws = []
    for qblk, listed, _ in units:
        kcat = jnp.concatenate([kv[0, e] for e in listed], axis=0)
        raws.append(lax.dot_general(qblk, kcat, (((1,), (1,)), ((), ())), preferred_element_type=jnp.float32))
    soft = [soften(raw, block) for raw, (_, _, block) in zip(raws, units)]
    done = []
    for (probs, total), (_, listed, _) in zip(soft, units):
        vcat = jnp.concatenate([kv[1, e] for e in listed], axis=0)
        done.append((jnp.dot(probs, vcat, preferred_element_type=jnp.float32) / total).astype(jnp.bfloat16))
    return done


def kernel(nc, nt, ratio, mult, lists, q, k, v, out, qh, kv, oh,
           s_kv, s_q, s_o, s_f, s_s, l_kv, l_o, r_kv, r_f, r_s, r_q, r_o):
    n = nc * nt
    rows = q.shape[0]
    per = rows // BLK
    c, t = lax.axis_index("seq"), lax.axis_index("tensor")
    me = c * nt + t
    sib = 1 - t

    def dev(chip, core):
        return {"seq": chip, "tensor": core}

    def part(index):
        return pl.ds(pl.multiple_of(index * rows, rows), rows)

    def blocks(index):
        return pl.ds(index * per, per)

    def cols(head):
        return pl.ds(pl.multiple_of(head * HD, HD), HD)

    def remote(src, dst, send, recv, chip, core):
        return pltpu.make_async_remote_copy(
            src_ref=src, dst_ref=dst, send_sem=send, recv_sem=recv,
            device_id=dev(chip, core), device_id_type=MESH,
        )

    def drain(ref, sem):
        pltpu.make_async_copy(ref, ref, sem).wait()

    def loop(start, stop, step):
        def run(i, _):
            step(i)
            return 0
        lax.fori_loop(start, stop, run, 0)

    barrier = pltpu.get_barrier_semaphore()

    def greet(i):
        p = lax.rem(me + i, n)
        pl.semaphore_signal(barrier, inc=1, device_id=dev(p // nt, lax.rem(p, nt)), device_id_type=MESH)

    loop(1, n, greet)
    pl.semaphore_wait(barrier, n - 1)

    def send_kv(j):
        dc = lax.rem(c + j * mult, nc)
        head = cols((dc * nt) // ratio)
        for core, src in ((0, k), (1, v)):
            remote(src.at[:, :, head], kv.at[core, blocks(me)], s_kv, r_kv.at[me], dc, core).start()

    loop(1, nc, send_kv)
    head = cols(me // ratio)
    local = []
    for core, src in ((0, k), (1, v)):
        remote(src.at[:, :, head], kv.at[core, blocks(me)], s_s.at[core], r_s.at[core], c, sib).start()
        local.append(pltpu.make_async_copy(src.at[:, :, head], kv.at[core, blocks(me)], l_kv.at[core]))
        local[-1].start()

    pltpu.make_async_copy(q.at[:, cols(me)], qh.at[part(me)], r_q.at[me]).start()
    remote(q.at[:, cols(c * nt + sib)], qh.at[part(me)], s_q, r_q.at[me], c, sib).start()

    def send_q(j):
        dc = lax.rem(c + j * mult, nc)
        for core in range(nt):
            remote(q.at[:, cols(dc * nt + core)], qh.at[part(me)], s_q, r_q.at[me], dc, core).start()

    loop(1, nc, send_q)

    def forward(j):
        sc = lax.rem(c + (nc - j) * mult, nc)
        for core in range(nt):
            s = sc * nt + core
            drain(kv.at[t, blocks(s)], r_kv.at[s])
            remote(kv.at[t, blocks(s)], kv.at[t, blocks(s)], s_f, r_f, c, sib).start()

    loop(1, nc, forward)
    for core in range(nt):
        local[core].wait()
        drain(kv.at[core, blocks(0)], r_s.at[core])
    drain(kv.at[0, pl.ds(0, (n - nt) * per)], r_f)

    def attend(i):
        j = i // nt
        sc = lax.rem(c + (nc - j) * mult, nc)
        score = lax.rem(t + i, nt)
        s = sc * nt + score
        drain(qh.at[part(s)], r_q.at[s])
        units, places = [], []
        for inner in range(per):
            block = s * per + inner
            places.append(pl.ds(pl.multiple_of(block * BLK, BLK), BLK))
            units.append((qh[places[-1], :], [lists[block * KSEL + e] for e in range(KSEL)], block))
        for here, made in zip(places, attend_units(kv, units)):
            oh[here, :] = made

        @pl.when(i == 0)
        def _():
            pltpu.make_async_copy(oh.at[part(s)], out.at[:, cols(me)], l_o).start()

        @pl.when(i > 0)
        def _():
            remote(oh.at[part(s)], out.at[:, cols(me)], s_o, r_o, sc, score).start()

    loop(0, n, attend)

    drain(oh.at[part(0)], l_o)
    others = pl.ds(0, (n - 1) * HD)
    drain(out.at[:, others], r_o)
    drain(out.at[:, others], s_o)
    drain(out.at[:, others], s_q)
    drain(kv.at[0, pl.ds(0, (n - nt) * per)], s_kv)
    drain(kv.at[0, pl.ds(0, (n - nt) * per)], s_f)
    for core in range(nt):
        drain(kv.at[core, blocks(0)], s_s.at[core])


def halves_kernel(nc, lists, q, k, v, out, lv, ls, qh, kva, kvb, oh,
                  s_l, r_l, c_l, s_own, s_up, s_q, s_o, s_f, s_s, l_kv, r_kv, r_f, r_s, r_q, r_o):
    nt = 2
    n = nc * nt
    half = nc // 2
    row = half // 2
    rows = q.shape[0]
    per = rows // BLK
    kvs = (kva, kvb)
    c, t = lax.axis_index("seq"), lax.axis_index("tensor")
    me = c * nt + t
    sib = 1 - t
    hz, cx = c // half, lax.rem(c, half)
    base = hz * half
    tz = cx // row
    mine = lax.rem(cx, row) * nt + t

    def dev(chip, core):
        return {"seq": chip, "tensor": core}

    def blocks(index):
        return pl.ds(index * per, per)

    def cols(index, width):
        return pl.ds(pl.multiple_of(index * width, width), width)

    def remote(src, dst, send, recv, chip, core):
        return pltpu.make_async_remote_copy(
            src_ref=src, dst_ref=dst, send_sem=send, recv_sem=recv,
            device_id=dev(chip, core), device_id_type=MESH,
        )

    def drain(ref, sem):
        pltpu.make_async_copy(ref, ref, sem).wait()

    def loop(start, stop, step):
        def run(i, _):
            step(i)
            return 0
        lax.fori_loop(start, stop, run, 0)

    barrier = pltpu.get_barrier_semaphore()

    def greet(i):
        p = lax.rem(me + i, n)
        pl.semaphore_signal(barrier, inc=1, device_id=dev(p // nt, lax.rem(p, nt)), device_id_type=MESH)

    loop(1, n, greet)
    pl.semaphore_wait(barrier, n - 1)

    def send_kv(j, dc, sem):
        at = cols((lax.rem(dc, half)) * 2 + j, HD)
        for core, src in ((0, k), (1, v)):
            remote(src.at[:, :, at], kvs[j].at[core, blocks(me)], sem, r_kv.at[j, me], dc, core).start()

    def send_up(j):
        @pl.when(hz == 0)
        def _():
            loop(0, half, lambda i: send_kv(j, half + lax.rem(cx + i, half), s_up))

    def send_own(j):
        loop(1, half, lambda i: send_kv(j, base + lax.rem(cx + i, half), s_own))
        at = cols(cx * 2 + j, HD)
        for core, src in ((0, k), (1, v)):
            remote(src.at[:, :, at], kvs[j].at[core, blocks(me)], s_s.at[j, core], r_s.at[j, core], c, sib).start()
            pltpu.make_async_copy(src.at[:, :, at], kvs[j].at[core, blocks(me)], l_kv.at[j, core]).start()

    entry = lax.rem(me, 4)
    for far in range(2):
        dc = far * half + me // 4
        for core in range(nt):
            itself = (dc == c) & (t == core)

            @pl.when(itself)
            def _():
                pltpu.make_async_copy(lists, lv.at[entry], r_l.at[entry]).start()

            @pl.when(jnp.logical_not(itself))
            def _():
                remote(lists, lv.at[entry], s_l.at[far, core], r_l.at[entry], dc, core).start()

    send_own(0)

    def send_q(i):
        cl = lax.rem(cx + i, half)
        remote(q.at[:, cols(cl, 4 * HD)], qh.at[mine], s_q, r_q.at[mine], base + cl, tz).start()

    @pl.when(tz == t)
    def _():
        pltpu.make_async_copy(q.at[:, cols(cx, 4 * HD)], qh.at[mine], r_q.at[mine]).start()

    @pl.when(tz != t)
    def _():
        send_q(0)

    loop(1, half, send_q)
    send_own(1)
    send_up(0)
    send_up(1)

    def forward(j, chip):
        for core in range(nt):
            here = kvs[j].at[t, blocks(chip * nt + core)]
            drain(here, r_kv.at[j, chip * nt + core])
            remote(here, here, s_f.at[j], r_f.at[j], c, sib).start()

    def forward_own(j):
        loop(1, half, lambda i: forward(j, base + lax.rem(cx + half - i, half)))

    def settle(j):
        for core in range(nt):
            drain(kvs[j].at[core, blocks(0)], r_s.at[j, core])
            drain(kvs[j].at[core, blocks(0)], l_kv.at[j, core])

        @pl.when(hz == 0)
        def _():
            drain(kvs[j].at[0, pl.ds(0, (half - 1) * nt * per)], r_f.at[j])

        @pl.when(hz == 1)
        def _():
            drain(kvs[j].at[0, pl.ds(0, (nc - 1) * nt * per)], r_f.at[j])

    forward_own(0)

    @pl.when(hz == 1)
    def _():
        loop(0, half, lambda i: forward(0, lax.rem(cx + half - i, half)))

    for e in range(4):
        drain(lv.at[e], r_l.at[e])
    pltpu.make_async_copy(lv, ls, c_l).start()
    settle(0)
    pltpu.make_async_copy(lv, ls, c_l).wait()

    def attend(j, i):
        slot = lax.rem(mine + i, 4)
        sc, score = base + t * row + slot // nt, lax.rem(slot, nt)
        if j == 0:
            drain(qh.at[slot], r_q.at[slot])
        units, places = [], []
        for inner in range(per):
            block = (sc * nt + score) * per + inner
            for one in range(2):
                head = 2 * j + one
                listed = [ls[head, e, 0, block] for e in range(KSEL)]
                here = pl.ds(inner * BLK, BLK)
                places.append((here, pl.ds(one * HD, HD)))
                units.append((qh[slot, here, pl.ds(head * HD, HD)], listed, block))
        for here, made in zip(places, attend_units(kvs[j], units)):
            oh[slot, j, here[0], here[1]] = made
        itself = (sc == c) & (score == t)
        goal = out.at[:, cols(cx * 2 + j, 2 * HD)]

        @pl.when(itself)
        def _():
            pltpu.make_async_copy(oh.at[slot, j], goal, r_o.at[cx, j]).start()

        @pl.when(jnp.logical_not(itself))
        def _():
            remote(oh.at[slot, j], goal, s_o, r_o.at[cx, j], sc, score).start()

    def first(i):
        @pl.when(i == 0)
        def _():
            forward_own(1)

        attend(0, i)

        @pl.when(hz == 1)
        def _():
            forward(1, lax.rem(cx + half - i, half))

    loop(0, 4, first)
    settle(1)
    loop(0, 4, lambda i: attend(1, i))

    for cl in range(half):
        for j in range(2):
            drain(out.at[:, pl.ds((cl * 2 + j) * 2 * HD, 2 * HD)], r_o.at[cl, j])

    @pl.when(tz == t)
    def _():
        drain(out.at[:, pl.ds(0, 3 * 4 * HD)], s_q)

    @pl.when(tz != t)
    def _():
        drain(out, s_q)

    @pl.when((base + t * row == c - lax.rem(cx, row)))
    def _():
        drain(out.at[:, pl.ds(0, 6 * 2 * HD)], s_o)

    @pl.when((base + t * row != c - lax.rem(cx, row)))
    def _():
        drain(out, s_o)

    drain(kva.at[0, pl.ds(0, (half - 1) * 4 * per)], s_own)

    @pl.when(hz == 0)
    def _():
        drain(kva.at[0], s_up)

    for j in range(2):
        @pl.when(hz == 0)
        def _():
            drain(kva.at[0, pl.ds(0, (half - 1) * nt * per)], s_f.at[j])

        @pl.when(hz == 1)
        def _():
            drain(kva.at[0, pl.ds(0, (nc - 1) * nt * per)], s_f.at[j])

        for core in range(nt):
            drain(kva.at[core, blocks(0)], s_s.at[j, core])

    for far in range(2):
        dc = far * half + me // 4
        for core in range(nt):
            @pl.when(jnp.logical_not((dc == c) & (t == core)))
            def _():
                drain(lv.at[0], s_l.at[far, core])


def halves(nc, queries, keys, values, block_lists):
    rows, width = queries.shape
    n = 2 * nc
    per = rows // BLK
    dma = pltpu.SemaphoreType.DMA
    hbm = pl.BlockSpec(memory_space=pl.ANY)
    entry = (KSEL, 1, block_lists.shape[1])
    kv = pltpu.VMEM((2, n * per, BLK, HD), jnp.bfloat16)
    return pl.pallas_call(
        functools.partial(halves_kernel, nc),
        out_shape=pltpu.VMEM((rows, width), jnp.bfloat16),
        in_specs=[hbm, hbm, hbm, hbm],
        out_specs=hbm,
        scratch_shapes=[
            pltpu.VMEM((4, *entry), jnp.int32),
            pltpu.SMEM((4, *entry), jnp.int32),
            pltpu.VMEM((4, rows, 4 * HD), jnp.bfloat16),
            kv,
            kv,
            pltpu.VMEM((4, 2, rows, 2 * HD), jnp.bfloat16),
            dma((2, 2)), dma((4,)), dma, dma, dma, dma, dma, dma((2,)), dma((2, 2)), dma((2, 2)),
            dma((2, n)), dma((2,)), dma((2, 2)), dma((4,)), dma((nc // 2, 2)),
        ],
        compiler_params=pltpu.CompilerParams(
            collective_id=0, has_side_effects=True, vmem_limit_bytes=VMEM_MIB * 2**20
        ),
        cost_estimate=pl.CostEstimate(
            flops=4 * n * rows * KSEL * BLK * HD, bytes_accessed=8 * n * rows * HD, transcendentals=n * rows * KSEL * BLK
        ),
    )(block_lists.transpose(2, 0, 1), queries, keys.reshape(per, BLK, -1), values.reshape(per, BLK, -1))


def body(nc, nt, queries, keys, values, block_lists):
    rows, width = queries.shape
    n = nc * nt
    heads = width // HD
    kv_heads = keys.shape[1] // HD
    ratio = heads // kv_heads
    assert nt == 2 and heads == n and ratio % nt == 0 and rows % BLK == 0
    if nc == 8 and ratio == 2:
        return halves(nc, queries, keys, values, block_lists)
    mult = nc // 2 - 1 if nc >= 4 and nc & (nc - 1) == 0 else 1
    dma, shape = pltpu.SemaphoreType.DMA, jax.ShapeDtypeStruct
    hbm = pl.BlockSpec(memory_space=pl.ANY)
    return pl.pallas_call(
        functools.partial(kernel, nc, nt, ratio, mult),
        out_shape=shape((rows, width), jnp.bfloat16),
        in_specs=[pl.BlockSpec(memory_space=pltpu.SMEM), hbm, hbm, hbm],
        out_specs=hbm,
        scratch_shapes=[
            pltpu.VMEM((n * rows, HD), jnp.bfloat16),
            pltpu.VMEM((2, n * rows // BLK, BLK, HD), jnp.bfloat16),
            pltpu.VMEM((n * rows, HD), jnp.bfloat16),
            dma, dma, dma, dma, dma((nt,)), dma((nt,)), dma,
            dma((n,)), dma, dma((nt,)), dma((n,)), dma,
        ],
        compiler_params=pltpu.CompilerParams(
            collective_id=0, has_side_effects=True, vmem_limit_bytes=40 * 2**20
        ),
        cost_estimate=pl.CostEstimate(
            flops=4 * n * rows * KSEL * BLK * HD, bytes_accessed=8 * n * rows * HD, transcendentals=n * rows * KSEL * BLK
        ),
    )(
        block_lists.reshape(-1),
        queries,
        keys.reshape(rows // BLK, BLK, kv_heads * HD),
        values.reshape(rows // BLK, BLK, kv_heads * HD),
    )


def solution(mesh):
    placed = (
        P(("groups", "seq", "tensor"), None),
        P(("groups", "seq", "tensor"), None),
        P(("groups", "seq", "tensor"), None),
        P(("seq", "tensor"), None, None),
    )
    return jax.shard_map(
        functools.partial(body, mesh.shape["seq"], mesh.shape["tensor"]),
        mesh=mesh,
        in_specs=placed,
        out_specs=P(("groups", "seq", "tensor"), None),
        check_vma=False,
    )
```

```python
import functools

import jax
import jax.numpy as jnp
from jax import lax
from jax.experimental import pallas as pl
from jax.experimental.pallas import tpu as pltpu
from jax.sharding import PartitionSpec as P

HD = 128
BLK = 64
KSEL = 12
VMEM_MIB = 60
MESH = pl.DeviceIdType.MESH
COEF = 1.4426950408889634 / (128.0**0.5)


def soften(raw, block):
    row = lax.broadcasted_iota(jnp.int32, raw.shape, 0)
    col = lax.broadcasted_iota(jnp.int32, raw.shape, 1)
    live = jnp.minimum(block + 1, KSEL) * BLK
    keep = ((col >= BLK) | (col <= row)) & (col < live)
    raw = jnp.where(keep, raw, jnp.float32(-1e30))
    top = jnp.max(raw, axis=1, keepdims=True)
    probs = jnp.exp2((raw - top) * jnp.float32(COEF))
    return probs.astype(jnp.bfloat16), jnp.sum(probs, axis=1, keepdims=True)


def attend_units(kv, units):
    raws = []
    for qblk, listed, _ in units:
        kcat = jnp.concatenate([kv[0, e] for e in listed], axis=0)
        raws.append(lax.dot_general(qblk, kcat, (((1,), (1,)), ((), ())), preferred_element_type=jnp.float32))
    soft = [soften(raw, block) for raw, (_, _, block) in zip(raws, units)]
    done = []
    for (probs, total), (_, listed, _) in zip(soft, units):
        vcat = jnp.concatenate([kv[1, e] for e in listed], axis=0)
        done.append((jnp.dot(probs, vcat, preferred_element_type=jnp.float32) / total).astype(jnp.bfloat16))
    return done


def kernel(nc, nt, ratio, mult, lists, q, k, v, out, qh, kv, oh,
           s_kv, s_q, s_o, s_f, s_s, l_kv, l_o, r_kv, r_f, r_s, r_q, r_o):
    n = nc * nt
    rows = q.shape[0]
    per = rows // BLK
    c, t = lax.axis_index("seq"), lax.axis_index("tensor")
    me = c * nt + t
    sib = 1 - t

    def dev(chip, core):
        return {"seq": chip, "tensor": core}

    def part(index):
        return pl.ds(pl.multiple_of(index * rows, rows), rows)

    def blocks(index):
        return pl.ds(index * per, per)

    def cols(head):
        return pl.ds(pl.multiple_of(head * HD, HD), HD)

    def remote(src, dst, send, recv, chip, core):
        return pltpu.make_async_remote_copy(
            src_ref=src, dst_ref=dst, send_sem=send, recv_sem=recv,
            device_id=dev(chip, core), device_id_type=MESH,
        )

    def drain(ref, sem):
        pltpu.make_async_copy(ref, ref, sem).wait()

    def loop(start, stop, step):
        def run(i, _):
            step(i)
            return 0
        lax.fori_loop(start, stop, run, 0)

    barrier = pltpu.get_barrier_semaphore()

    def greet(i):
        p = lax.rem(me + i, n)
        pl.semaphore_signal(barrier, inc=1, device_id=dev(p // nt, lax.rem(p, nt)), device_id_type=MESH)

    loop(1, n, greet)
    pl.semaphore_wait(barrier, n - 1)

    def send_kv(j):
        dc = lax.rem(c + j * mult, nc)
        head = cols((dc * nt) // ratio)
        for core, src in ((0, k), (1, v)):
            remote(src.at[:, :, head], kv.at[core, blocks(me)], s_kv, r_kv.at[me], dc, core).start()

    loop(1, nc, send_kv)
    head = cols(me // ratio)
    local = []
    for core, src in ((0, k), (1, v)):
        remote(src.at[:, :, head], kv.at[core, blocks(me)], s_s.at[core], r_s.at[core], c, sib).start()
        local.append(pltpu.make_async_copy(src.at[:, :, head], kv.at[core, blocks(me)], l_kv.at[core]))
        local[-1].start()

    pltpu.make_async_copy(q.at[:, cols(me)], qh.at[part(me)], r_q.at[me]).start()
    remote(q.at[:, cols(c * nt + sib)], qh.at[part(me)], s_q, r_q.at[me], c, sib).start()

    def send_q(j):
        dc = lax.rem(c + j * mult, nc)
        for core in range(nt):
            remote(q.at[:, cols(dc * nt + core)], qh.at[part(me)], s_q, r_q.at[me], dc, core).start()

    loop(1, nc, send_q)

    def forward(j):
        sc = lax.rem(c + (nc - j) * mult, nc)
        for core in range(nt):
            s = sc * nt + core
            drain(kv.at[t, blocks(s)], r_kv.at[s])
            remote(kv.at[t, blocks(s)], kv.at[t, blocks(s)], s_f, r_f, c, sib).start()

    loop(1, nc, forward)
    for core in range(nt):
        local[core].wait()
        drain(kv.at[core, blocks(0)], r_s.at[core])
    drain(kv.at[0, pl.ds(0, (n - nt) * per)], r_f)

    def attend(i):
        j = i // nt
        sc = lax.rem(c + (nc - j) * mult, nc)
        score = lax.rem(t + i, nt)
        s = sc * nt + score
        drain(qh.at[part(s)], r_q.at[s])
        units, places = [], []
        for inner in range(per):
            block = s * per + inner
            places.append(pl.ds(pl.multiple_of(block * BLK, BLK), BLK))
            units.append((qh[places[-1], :], [lists[block * KSEL + e] for e in range(KSEL)], block))
        for here, made in zip(places, attend_units(kv, units)):
            oh[here, :] = made

        @pl.when(i == 0)
        def _():
            pltpu.make_async_copy(oh.at[part(s)], out.at[:, cols(me)], l_o).start()

        @pl.when(i > 0)
        def _():
            remote(oh.at[part(s)], out.at[:, cols(me)], s_o, r_o, sc, score).start()

    loop(0, n, attend)

    drain(oh.at[part(0)], l_o)
    others = pl.ds(0, (n - 1) * HD)
    drain(out.at[:, others], r_o)
    drain(out.at[:, others], s_o)
    drain(out.at[:, others], s_q)
    drain(kv.at[0, pl.ds(0, (n - nt) * per)], s_kv)
    drain(kv.at[0, pl.ds(0, (n - nt) * per)], s_f)
    for core in range(nt):
        drain(kv.at[core, blocks(0)], s_s.at[core])


def halves_kernel(nc, lists, q, k, v, out, lv, ls, qh, kva, kvb, oh,
                  s_l, r_l, c_l, s_own, s_up, s_q, s_o, s_f, s_s, l_kv, r_kv, r_f, r_s, r_q, r_o):
    nt = 2
    n = nc * nt
    half = nc // 2
    row = half // 2
    rows = q.shape[0]
    per = rows // BLK
    kvs = (kva, kvb)
    c, t = lax.axis_index("seq"), lax.axis_index("tensor")
    me = c * nt + t
    sib = 1 - t
    hz, cx = c // half, lax.rem(c, half)
    base = hz * half
    tz = cx // row
    mine = lax.rem(cx, row) * nt + t

    def dev(chip, core):
        return {"seq": chip, "tensor": core}

    def blocks(index):
        return pl.ds(index * per, per)

    def cols(index, width):
        return pl.ds(pl.multiple_of(index * width, width), width)

    def remote(src, dst, send, recv, chip, core):
        return pltpu.make_async_remote_copy(
            src_ref=src, dst_ref=dst, send_sem=send, recv_sem=recv,
            device_id=dev(chip, core), device_id_type=MESH,
        )

    def drain(ref, sem):
        pltpu.make_async_copy(ref, ref, sem).wait()

    def loop(start, stop, step):
        def run(i, _):
            step(i)
            return 0
        lax.fori_loop(start, stop, run, 0)

    barrier = pltpu.get_barrier_semaphore()

    def greet(i):
        p = lax.rem(me + i, n)
        pl.semaphore_signal(barrier, inc=1, device_id=dev(p // nt, lax.rem(p, nt)), device_id_type=MESH)

    loop(1, n, greet)
    pl.semaphore_wait(barrier, n - 1)

    def send_kv(j, dc, sem):
        at = cols((lax.rem(dc, half)) * 2 + j, HD)
        for core, src in ((0, k), (1, v)):
            remote(src.at[:, :, at], kvs[j].at[core, blocks(me)], sem, r_kv.at[j, me], dc, core).start()

    def send_up(j):
        @pl.when(hz == 0)
        def _():
            loop(0, half, lambda i: send_kv(j, half + lax.rem(cx + i, half), s_up))

    def send_own(j):
        loop(1, half, lambda i: send_kv(j, base + lax.rem(cx + i, half), s_own))
        at = cols(cx * 2 + j, HD)
        for core, src in ((0, k), (1, v)):
            remote(src.at[:, :, at], kvs[j].at[core, blocks(me)], s_s.at[j, core], r_s.at[j, core], c, sib).start()
            pltpu.make_async_copy(src.at[:, :, at], kvs[j].at[core, blocks(me)], l_kv.at[j, core]).start()

    entry = lax.rem(me, 4)
    for far in range(2):
        dc = far * half + me // 4
        for core in range(nt):
            itself = (dc == c) & (t == core)

            @pl.when(itself)
            def _():
                pltpu.make_async_copy(lists, lv.at[entry], r_l.at[entry]).start()

            @pl.when(jnp.logical_not(itself))
            def _():
                remote(lists, lv.at[entry], s_l.at[far, core], r_l.at[entry], dc, core).start()

    send_own(0)

    def send_q(i):
        cl = lax.rem(cx + i, half)
        remote(q.at[:, cols(cl, 4 * HD)], qh.at[mine], s_q, r_q.at[mine], base + cl, tz).start()

    @pl.when(tz == t)
    def _():
        pltpu.make_async_copy(q.at[:, cols(cx, 4 * HD)], qh.at[mine], r_q.at[mine]).start()

    @pl.when(tz != t)
    def _():
        send_q(0)

    loop(1, half, send_q)
    send_own(1)
    send_up(0)
    send_up(1)

    def forward(j, chip):
        for core in range(nt):
            here = kvs[j].at[t, blocks(chip * nt + core)]
            drain(here, r_kv.at[j, chip * nt + core])
            remote(here, here, s_f.at[j], r_f.at[j], c, sib).start()

    def forward_own(j):
        loop(1, half, lambda i: forward(j, base + lax.rem(cx + half - i, half)))

    def settle(j):
        for core in range(nt):
            drain(kvs[j].at[core, blocks(0)], r_s.at[j, core])
            drain(kvs[j].at[core, blocks(0)], l_kv.at[j, core])

        @pl.when(hz == 0)
        def _():
            drain(kvs[j].at[0, pl.ds(0, (half - 1) * nt * per)], r_f.at[j])

        @pl.when(hz == 1)
        def _():
            drain(kvs[j].at[0, pl.ds(0, (nc - 1) * nt * per)], r_f.at[j])

    forward_own(0)

    @pl.when(hz == 1)
    def _():
        loop(0, half, lambda i: forward(0, lax.rem(cx + half - i, half)))

    for e in range(4):
        drain(lv.at[e], r_l.at[e])
    pltpu.make_async_copy(lv, ls, c_l).start()
    settle(0)
    pltpu.make_async_copy(lv, ls, c_l).wait()

    def attend(j, i):
        slot = lax.rem(mine // nt + 1 + i // nt, 2) * nt + lax.rem(t + 1 + i, nt)
        sc, score = base + t * row + slot // nt, lax.rem(slot, nt)
        if j == 0:
            drain(qh.at[slot], r_q.at[slot])
        units, places = [], []
        for inner in range(per):
            block = (sc * nt + score) * per + inner
            for one in range(2):
                head = 2 * j + one
                listed = [ls[head, e, 0, block] for e in range(KSEL)]
                here = pl.ds(inner * BLK, BLK)
                places.append((here, pl.ds(one * HD, HD)))
                units.append((qh[slot, here, pl.ds(head * HD, HD)], listed, block))
        for here, made in zip(places, attend_units(kvs[j], units)):
            oh[slot, j, here[0], here[1]] = made
        itself = (sc == c) & (score == t)
        goal = out.at[:, cols(cx * 2 + j, 2 * HD)]

        @pl.when(itself)
        def _():
            pltpu.make_async_copy(oh.at[slot, j], goal, r_o.at[cx, j]).start()

        @pl.when(jnp.logical_not(itself))
        def _():
            remote(oh.at[slot, j], goal, s_o, r_o.at[cx, j], sc, score).start()

    def first(i):
        @pl.when(i == 0)
        def _():
            forward_own(1)

        attend(0, i)

        @pl.when(hz == 1)
        def _():
            forward(1, lax.rem(cx + half - i, half))

    loop(0, 4, first)
    settle(1)
    loop(0, 4, lambda i: attend(1, i))

    for cl in range(half):
        for j in range(2):
            drain(out.at[:, pl.ds((cl * 2 + j) * 2 * HD, 2 * HD)], r_o.at[cl, j])

    @pl.when(tz == t)
    def _():
        drain(out.at[:, pl.ds(0, 3 * 4 * HD)], s_q)

    @pl.when(tz != t)
    def _():
        drain(out, s_q)

    @pl.when((base + t * row == c - lax.rem(cx, row)))
    def _():
        drain(out.at[:, pl.ds(0, 6 * 2 * HD)], s_o)

    @pl.when((base + t * row != c - lax.rem(cx, row)))
    def _():
        drain(out, s_o)

    drain(kva.at[0, pl.ds(0, (half - 1) * 4 * per)], s_own)

    @pl.when(hz == 0)
    def _():
        drain(kva.at[0], s_up)

    for j in range(2):
        @pl.when(hz == 0)
        def _():
            drain(kva.at[0, pl.ds(0, (half - 1) * nt * per)], s_f.at[j])

        @pl.when(hz == 1)
        def _():
            drain(kva.at[0, pl.ds(0, (nc - 1) * nt * per)], s_f.at[j])

        for core in range(nt):
            drain(kva.at[core, blocks(0)], s_s.at[j, core])

    for far in range(2):
        dc = far * half + me // 4
        for core in range(nt):
            @pl.when(jnp.logical_not((dc == c) & (t == core)))
            def _():
                drain(lv.at[0], s_l.at[far, core])


def halves(nc, queries, keys, values, block_lists):
    rows, width = queries.shape
    n = 2 * nc
    per = rows // BLK
    dma = pltpu.SemaphoreType.DMA
    hbm = pl.BlockSpec(memory_space=pl.ANY)
    entry = (KSEL, 1, block_lists.shape[1])
    kv = pltpu.VMEM((2, n * per, BLK, HD), jnp.bfloat16)
    return pl.pallas_call(
        functools.partial(halves_kernel, nc),
        out_shape=pltpu.VMEM((rows, width), jnp.bfloat16),
        in_specs=[hbm, hbm, hbm, hbm],
        out_specs=hbm,
        scratch_shapes=[
            pltpu.VMEM((4, *entry), jnp.int32),
            pltpu.SMEM((4, *entry), jnp.int32),
            pltpu.VMEM((4, rows, 4 * HD), jnp.bfloat16),
            kv,
            kv,
            pltpu.VMEM((4, 2, rows, 2 * HD), jnp.bfloat16),
            dma((2, 2)), dma((4,)), dma, dma, dma, dma, dma, dma((2,)), dma((2, 2)), dma((2, 2)),
            dma((2, n)), dma((2,)), dma((2, 2)), dma((4,)), dma((nc // 2, 2)),
        ],
        compiler_params=pltpu.CompilerParams(
            collective_id=0, has_side_effects=True, vmem_limit_bytes=VMEM_MIB * 2**20
        ),
        cost_estimate=pl.CostEstimate(
            flops=4 * n * rows * KSEL * BLK * HD, bytes_accessed=8 * n * rows * HD, transcendentals=n * rows * KSEL * BLK
        ),
    )(block_lists.transpose(2, 0, 1), queries, keys.reshape(per, BLK, -1), values.reshape(per, BLK, -1))


def body(nc, nt, queries, keys, values, block_lists):
    rows, width = queries.shape
    n = nc * nt
    heads = width // HD
    kv_heads = keys.shape[1] // HD
    ratio = heads // kv_heads
    assert nt == 2 and heads == n and ratio % nt == 0 and rows % BLK == 0
    if nc == 8 and ratio == 2:
        return halves(nc, queries, keys, values, block_lists)
    mult = nc // 2 - 1 if nc >= 4 and nc & (nc - 1) == 0 else 1
    dma, shape = pltpu.SemaphoreType.DMA, jax.ShapeDtypeStruct
    hbm = pl.BlockSpec(memory_space=pl.ANY)
    return pl.pallas_call(
        functools.partial(kernel, nc, nt, ratio, mult),
        out_shape=shape((rows, width), jnp.bfloat16),
        in_specs=[pl.BlockSpec(memory_space=pltpu.SMEM), hbm, hbm, hbm],
        out_specs=hbm,
        scratch_shapes=[
            pltpu.VMEM((n * rows, HD), jnp.bfloat16),
            pltpu.VMEM((2, n * rows // BLK, BLK, HD), jnp.bfloat16),
            pltpu.VMEM((n * rows, HD), jnp.bfloat16),
            dma, dma, dma, dma, dma((nt,)), dma((nt,)), dma,
            dma((n,)), dma, dma((nt,)), dma((n,)), dma,
        ],
        compiler_params=pltpu.CompilerParams(
            collective_id=0, has_side_effects=True, vmem_limit_bytes=40 * 2**20
        ),
        cost_estimate=pl.CostEstimate(
            flops=4 * n * rows * KSEL * BLK * HD, bytes_accessed=8 * n * rows * HD, transcendentals=n * rows * KSEL * BLK
        ),
    )(
        block_lists.reshape(-1),
        queries,
        keys.reshape(rows // BLK, BLK, kv_heads * HD),
        values.reshape(rows // BLK, BLK, kv_heads * HD),
    )


def solution(mesh):
    placed = (
        P(("groups", "seq", "tensor"), None),
        P(("groups", "seq", "tensor"), None),
        P(("groups", "seq", "tensor"), None),
        P(("seq", "tensor"), None, None),
    )
    return jax.shard_map(
        functools.partial(body, mesh.shape["seq"], mesh.shape["tensor"]),
        mesh=mesh,
        in_specs=placed,
        out_specs=P(("groups", "seq", "tensor"), None),
        check_vma=False,
    )
```

```python
import functools

import jax
import jax.numpy as jnp
from jax import lax
from jax.experimental import pallas as pl
from jax.experimental.pallas import tpu as pltpu
from jax.sharding import PartitionSpec as P

HD = 128
BLK = 64
KSEL = 12
VMEM_MIB = 60
MESH = pl.DeviceIdType.MESH
COEF = 1.4426950408889634 / (128.0**0.5)


def soften(raw, block):
    live = jnp.minimum(block + 1, KSEL) * BLK
    first, rest = raw[:, : 2 * BLK], raw[:, 2 * BLK :]
    row = lax.broadcasted_iota(jnp.int32, first.shape, 0)
    col = lax.broadcasted_iota(jnp.int32, first.shape, 1)
    keep = ((col >= BLK) | (col <= row)) & (col < live)
    later = lax.broadcasted_iota(jnp.int32, rest.shape, 1) < live - 2 * BLK
    first = jnp.where(keep, first, jnp.float32(-1e30))
    rest = jnp.where(later, rest, jnp.float32(-1e30))
    raw = jnp.concatenate([first, rest], axis=1)
    top = jnp.max(raw, axis=1, keepdims=True)
    probs = jnp.exp2((raw - top) * jnp.float32(COEF))
    return probs.astype(jnp.bfloat16), jnp.sum(probs, axis=1, keepdims=True)


def attend_units(kv, units):
    raws = []
    for qblk, listed, _ in units:
        kcat = jnp.concatenate([kv[0, e] for e in listed], axis=0)
        raws.append(lax.dot_general(qblk, kcat, (((1,), (1,)), ((), ())), preferred_element_type=jnp.float32))
    soft = [soften(raw, block) for raw, (_, _, block) in zip(raws, units)]
    done = []
    for (probs, total), (_, listed, _) in zip(soft, units):
        vcat = jnp.concatenate([kv[1, e] for e in listed], axis=0)
        done.append((jnp.dot(probs, vcat, preferred_element_type=jnp.float32) / total).astype(jnp.bfloat16))
    return done


def kernel(nc, nt, ratio, mult, lists, q, k, v, out, qh, kv, oh,
           s_kv, s_q, s_o, s_f, s_s, l_kv, l_o, r_kv, r_f, r_s, r_q, r_o):
    n = nc * nt
    rows = q.shape[0]
    per = rows // BLK
    c, t = lax.axis_index("seq"), lax.axis_index("tensor")
    me = c * nt + t
    sib = 1 - t

    def dev(chip, core):
        return {"seq": chip, "tensor": core}

    def part(index):
        return pl.ds(pl.multiple_of(index * rows, rows), rows)

    def blocks(index):
        return pl.ds(index * per, per)

    def cols(head):
        return pl.ds(pl.multiple_of(head * HD, HD), HD)

    def remote(src, dst, send, recv, chip, core):
        return pltpu.make_async_remote_copy(
            src_ref=src, dst_ref=dst, send_sem=send, recv_sem=recv,
            device_id=dev(chip, core), device_id_type=MESH,
        )

    def drain(ref, sem):
        pltpu.make_async_copy(ref, ref, sem).wait()

    def loop(start, stop, step):
        def run(i, _):
            step(i)
            return 0
        lax.fori_loop(start, stop, run, 0)

    barrier = pltpu.get_barrier_semaphore()

    def greet(i):
        p = lax.rem(me + i, n)
        pl.semaphore_signal(barrier, inc=1, device_id=dev(p // nt, lax.rem(p, nt)), device_id_type=MESH)

    loop(1, n, greet)
    pl.semaphore_wait(barrier, n - 1)

    def send_kv(j):
        dc = lax.rem(c + j * mult, nc)
        head = cols((dc * nt) // ratio)
        for core, src in ((0, k), (1, v)):
            remote(src.at[:, :, head], kv.at[core, blocks(me)], s_kv, r_kv.at[me], dc, core).start()

    loop(1, nc, send_kv)
    head = cols(me // ratio)
    local = []
    for core, src in ((0, k), (1, v)):
        remote(src.at[:, :, head], kv.at[core, blocks(me)], s_s.at[core], r_s.at[core], c, sib).start()
        local.append(pltpu.make_async_copy(src.at[:, :, head], kv.at[core, blocks(me)], l_kv.at[core]))
        local[-1].start()

    pltpu.make_async_copy(q.at[:, cols(me)], qh.at[part(me)], r_q.at[me]).start()
    remote(q.at[:, cols(c * nt + sib)], qh.at[part(me)], s_q, r_q.at[me], c, sib).start()

    def send_q(j):
        dc = lax.rem(c + j * mult, nc)
        for core in range(nt):
            remote(q.at[:, cols(dc * nt + core)], qh.at[part(me)], s_q, r_q.at[me], dc, core).start()

    loop(1, nc, send_q)

    def forward(j):
        sc = lax.rem(c + (nc - j) * mult, nc)
        for core in range(nt):
            s = sc * nt + core
            drain(kv.at[t, blocks(s)], r_kv.at[s])
            remote(kv.at[t, blocks(s)], kv.at[t, blocks(s)], s_f, r_f, c, sib).start()

    loop(1, nc, forward)
    for core in range(nt):
        local[core].wait()
        drain(kv.at[core, blocks(0)], r_s.at[core])
    drain(kv.at[0, pl.ds(0, (n - nt) * per)], r_f)

    def attend(i):
        j = i // nt
        sc = lax.rem(c + (nc - j) * mult, nc)
        score = lax.rem(t + i, nt)
        s = sc * nt + score
        drain(qh.at[part(s)], r_q.at[s])
        units, places = [], []
        for inner in range(per):
            block = s * per + inner
            places.append(pl.ds(pl.multiple_of(block * BLK, BLK), BLK))
            units.append((qh[places[-1], :], [lists[block * KSEL + e] for e in range(KSEL)], block))
        for here, made in zip(places, attend_units(kv, units)):
            oh[here, :] = made

        @pl.when(i == 0)
        def _():
            pltpu.make_async_copy(oh.at[part(s)], out.at[:, cols(me)], l_o).start()

        @pl.when(i > 0)
        def _():
            remote(oh.at[part(s)], out.at[:, cols(me)], s_o, r_o, sc, score).start()

    loop(0, n, attend)

    drain(oh.at[part(0)], l_o)
    others = pl.ds(0, (n - 1) * HD)
    drain(out.at[:, others], r_o)
    drain(out.at[:, others], s_o)
    drain(out.at[:, others], s_q)
    drain(kv.at[0, pl.ds(0, (n - nt) * per)], s_kv)
    drain(kv.at[0, pl.ds(0, (n - nt) * per)], s_f)
    for core in range(nt):
        drain(kv.at[core, blocks(0)], s_s.at[core])


def halves_kernel(nc, lists, q, k, v, out, lv, ls, qh, kva, kvb, oh,
                  s_l, r_l, c_l, s_own, s_up, s_q, s_o, s_f, s_s, l_kv, r_kv, r_f, r_s, r_q, r_o):
    nt = 2
    n = nc * nt
    half = nc // 2
    row = half // 2
    rows = q.shape[0]
    per = rows // BLK
    kvs = (kva, kvb)
    c, t = lax.axis_index("seq"), lax.axis_index("tensor")
    me = c * nt + t
    sib = 1 - t
    hz, cx = c // half, lax.rem(c, half)
    base = hz * half
    tz = cx // row
    mine = lax.rem(cx, row) * nt + t

    def dev(chip, core):
        return {"seq": chip, "tensor": core}

    def blocks(index):
        return pl.ds(index * per, per)

    def cols(index, width):
        return pl.ds(pl.multiple_of(index * width, width), width)

    def remote(src, dst, send, recv, chip, core):
        return pltpu.make_async_remote_copy(
            src_ref=src, dst_ref=dst, send_sem=send, recv_sem=recv,
            device_id=dev(chip, core), device_id_type=MESH,
        )

    def drain(ref, sem):
        pltpu.make_async_copy(ref, ref, sem).wait()

    def loop(start, stop, step):
        def run(i, _):
            step(i)
            return 0
        lax.fori_loop(start, stop, run, 0)

    barrier = pltpu.get_barrier_semaphore()

    def greet(i):
        p = lax.rem(me + i, n)
        pl.semaphore_signal(barrier, inc=1, device_id=dev(p // nt, lax.rem(p, nt)), device_id_type=MESH)

    loop(1, n, greet)
    pl.semaphore_wait(barrier, n - 1)

    def send_kv(j, dc, sem):
        at = cols((lax.rem(dc, half)) * 2 + j, HD)
        for core, src in ((0, k), (1, v)):
            remote(src.at[:, :, at], kvs[j].at[core, blocks(me)], sem, r_kv.at[j, me], dc, core).start()

    def send_up(j):
        @pl.when(hz == 0)
        def _():
            loop(0, half, lambda i: send_kv(j, half + lax.rem(cx + i, half), s_up))

    def send_own(j):
        loop(1, half, lambda i: send_kv(j, base + lax.rem(cx + i, half), s_own))
        at = cols(cx * 2 + j, HD)
        for core, src in ((0, k), (1, v)):
            remote(src.at[:, :, at], kvs[j].at[core, blocks(me)], s_s.at[j, core], r_s.at[j, core], c, sib).start()
            pltpu.make_async_copy(src.at[:, :, at], kvs[j].at[core, blocks(me)], l_kv.at[j, core]).start()

    entry = lax.rem(me, 4)
    for far in range(2):
        dc = far * half + me // 4
        for core in range(nt):
            itself = (dc == c) & (t == core)

            @pl.when(itself)
            def _():
                pltpu.make_async_copy(lists, lv.at[entry], r_l.at[entry]).start()

            @pl.when(jnp.logical_not(itself))
            def _():
                remote(lists, lv.at[entry], s_l.at[far, core], r_l.at[entry], dc, core).start()

    send_own(0)

    def send_q(i):
        cl = lax.rem(cx + i, half)
        remote(q.at[:, cols(cl, 4 * HD)], qh.at[mine], s_q, r_q.at[mine], base + cl, tz).start()

    @pl.when(tz == t)
    def _():
        pltpu.make_async_copy(q.at[:, cols(cx, 4 * HD)], qh.at[mine], r_q.at[mine]).start()

    @pl.when(tz != t)
    def _():
        send_q(0)

    loop(1, half, send_q)
    send_own(1)
    send_up(0)
    send_up(1)

    def forward(j, chip):
        for core in range(nt):
            here = kvs[j].at[t, blocks(chip * nt + core)]
            drain(here, r_kv.at[j, chip * nt + core])
            remote(here, here, s_f.at[j], r_f.at[j], c, sib).start()

    def forward_own(j):
        loop(1, half, lambda i: forward(j, base + lax.rem(cx + half - i, half)))

    def settle(j):
        for core in range(nt):
            drain(kvs[j].at[core, blocks(0)], r_s.at[j, core])
            drain(kvs[j].at[core, blocks(0)], l_kv.at[j, core])

        @pl.when(hz == 0)
        def _():
            drain(kvs[j].at[0, pl.ds(0, (half - 1) * nt * per)], r_f.at[j])

        @pl.when(hz == 1)
        def _():
            drain(kvs[j].at[0, pl.ds(0, (nc - 1) * nt * per)], r_f.at[j])

    forward_own(0)

    @pl.when(hz == 1)
    def _():
        loop(0, half, lambda i: forward(0, lax.rem(cx + half - i, half)))

    for e in range(4):
        drain(lv.at[e], r_l.at[e])
    pltpu.make_async_copy(lv, ls, c_l).start()
    settle(0)
    pltpu.make_async_copy(lv, ls, c_l).wait()

    def attend(j, i):
        slot = lax.rem(mine // nt + 1 + i // nt, 2) * nt + lax.rem(t + 1 + i, nt)
        sc, score = base + t * row + slot // nt, lax.rem(slot, nt)
        if j == 0:
            drain(qh.at[slot], r_q.at[slot])
        units, places = [], []
        for inner in range(per):
            block = (sc * nt + score) * per + inner
            for one in range(2):
                head = 2 * j + one
                listed = [ls[head, e, 0, block] for e in range(KSEL)]
                here = pl.ds(inner * BLK, BLK)
                places.append((here, pl.ds(one * HD, HD)))
                units.append((qh[slot, here, pl.ds(head * HD, HD)], listed, block))
        for here, made in zip(places, attend_units(kvs[j], units)):
            oh[slot, j, here[0], here[1]] = made
        itself = (sc == c) & (score == t)
        goal = out.at[:, cols(cx * 2 + j, 2 * HD)]

        @pl.when(itself)
        def _():
            pltpu.make_async_copy(oh.at[slot, j], goal, r_o.at[cx, j]).start()

        @pl.when(jnp.logical_not(itself))
        def _():
            remote(oh.at[slot, j], goal, s_o, r_o.at[cx, j], sc, score).start()

    def first(i):
        @pl.when(i == 0)
        def _():
            forward_own(1)

        attend(0, i)

        @pl.when(hz == 1)
        def _():
            forward(1, lax.rem(cx + half - i, half))

    loop(0, 4, first)
    settle(1)
    loop(0, 4, lambda i: attend(1, i))

    for cl in range(half):
        for j in range(2):
            drain(out.at[:, pl.ds((cl * 2 + j) * 2 * HD, 2 * HD)], r_o.at[cl, j])

    @pl.when(tz == t)
    def _():
        drain(out.at[:, pl.ds(0, 3 * 4 * HD)], s_q)

    @pl.when(tz != t)
    def _():
        drain(out, s_q)

    @pl.when((base + t * row == c - lax.rem(cx, row)))
    def _():
        drain(out.at[:, pl.ds(0, 6 * 2 * HD)], s_o)

    @pl.when((base + t * row != c - lax.rem(cx, row)))
    def _():
        drain(out, s_o)

    drain(kva.at[0, pl.ds(0, (half - 1) * 4 * per)], s_own)

    @pl.when(hz == 0)
    def _():
        drain(kva.at[0], s_up)

    for j in range(2):
        @pl.when(hz == 0)
        def _():
            drain(kva.at[0, pl.ds(0, (half - 1) * nt * per)], s_f.at[j])

        @pl.when(hz == 1)
        def _():
            drain(kva.at[0, pl.ds(0, (nc - 1) * nt * per)], s_f.at[j])

        for core in range(nt):
            drain(kva.at[core, blocks(0)], s_s.at[j, core])

    for far in range(2):
        dc = far * half + me // 4
        for core in range(nt):
            @pl.when(jnp.logical_not((dc == c) & (t == core)))
            def _():
                drain(lv.at[0], s_l.at[far, core])


def halves(nc, queries, keys, values, block_lists):
    rows, width = queries.shape
    n = 2 * nc
    per = rows // BLK
    dma = pltpu.SemaphoreType.DMA
    hbm = pl.BlockSpec(memory_space=pl.ANY)
    entry = (KSEL, 1, block_lists.shape[1])
    kv = pltpu.VMEM((2, n * per, BLK, HD), jnp.bfloat16)
    return pl.pallas_call(
        functools.partial(halves_kernel, nc),
        out_shape=pltpu.VMEM((rows, width), jnp.bfloat16),
        in_specs=[hbm, hbm, hbm, hbm],
        out_specs=hbm,
        scratch_shapes=[
            pltpu.VMEM((4, *entry), jnp.int32),
            pltpu.SMEM((4, *entry), jnp.int32),
            pltpu.VMEM((4, rows, 4 * HD), jnp.bfloat16),
            kv,
            kv,
            pltpu.VMEM((4, 2, rows, 2 * HD), jnp.bfloat16),
            dma((2, 2)), dma((4,)), dma, dma, dma, dma, dma, dma((2,)), dma((2, 2)), dma((2, 2)),
            dma((2, n)), dma((2,)), dma((2, 2)), dma((4,)), dma((nc // 2, 2)),
        ],
        compiler_params=pltpu.CompilerParams(
            collective_id=0, has_side_effects=True, vmem_limit_bytes=VMEM_MIB * 2**20
        ),
        cost_estimate=pl.CostEstimate(
            flops=4 * n * rows * KSEL * BLK * HD, bytes_accessed=8 * n * rows * HD, transcendentals=n * rows * KSEL * BLK
        ),
    )(block_lists.transpose(2, 0, 1), queries, keys.reshape(per, BLK, -1), values.reshape(per, BLK, -1))


def body(nc, nt, queries, keys, values, block_lists):
    rows, width = queries.shape
    n = nc * nt
    heads = width // HD
    kv_heads = keys.shape[1] // HD
    ratio = heads // kv_heads
    assert nt == 2 and heads == n and ratio % nt == 0 and rows % BLK == 0
    if nc == 8 and ratio == 2:
        return halves(nc, queries, keys, values, block_lists)
    mult = nc // 2 - 1 if nc >= 4 and nc & (nc - 1) == 0 else 1
    dma, shape = pltpu.SemaphoreType.DMA, jax.ShapeDtypeStruct
    hbm = pl.BlockSpec(memory_space=pl.ANY)
    return pl.pallas_call(
        functools.partial(kernel, nc, nt, ratio, mult),
        out_shape=shape((rows, width), jnp.bfloat16),
        in_specs=[pl.BlockSpec(memory_space=pltpu.SMEM), hbm, hbm, hbm],
        out_specs=hbm,
        scratch_shapes=[
            pltpu.VMEM((n * rows, HD), jnp.bfloat16),
            pltpu.VMEM((2, n * rows // BLK, BLK, HD), jnp.bfloat16),
            pltpu.VMEM((n * rows, HD), jnp.bfloat16),
            dma, dma, dma, dma, dma((nt,)), dma((nt,)), dma,
            dma((n,)), dma, dma((nt,)), dma((n,)), dma,
        ],
        compiler_params=pltpu.CompilerParams(
            collective_id=0, has_side_effects=True, vmem_limit_bytes=40 * 2**20
        ),
        cost_estimate=pl.CostEstimate(
            flops=4 * n * rows * KSEL * BLK * HD, bytes_accessed=8 * n * rows * HD, transcendentals=n * rows * KSEL * BLK
        ),
    )(
        block_lists.reshape(-1),
        queries,
        keys.reshape(rows // BLK, BLK, kv_heads * HD),
        values.reshape(rows // BLK, BLK, kv_heads * HD),
    )


def solution(mesh):
    placed = (
        P(("groups", "seq", "tensor"), None),
        P(("groups", "seq", "tensor"), None),
        P(("groups", "seq", "tensor"), None),
        P(("seq", "tensor"), None, None),
    )
    return jax.shard_map(
        functools.partial(body, mesh.shape["seq"], mesh.shape["tensor"]),
        mesh=mesh,
        in_specs=placed,
        out_specs=P(("groups", "seq", "tensor"), None),
        check_vma=False,
    )
```

```python
import functools

import jax
import jax.numpy as jnp
from jax import lax
from jax.experimental import pallas as pl
from jax.experimental.pallas import tpu as pltpu
from jax.sharding import PartitionSpec as P

HD = 128
BLK = 64
KSEL = 12
VMEM_MIB = 60
MESH = pl.DeviceIdType.MESH
COEF = 1.4426950408889634 / (128.0**0.5)


def soften(raw, block):
    row = lax.broadcasted_iota(jnp.int32, raw.shape, 0)
    col = lax.broadcasted_iota(jnp.int32, raw.shape, 1)
    live = jnp.minimum(block + 1, KSEL) * BLK
    keep = ((col >= BLK) | (col <= row)) & (col < live)
    raw = jnp.where(keep, raw, jnp.float32(-1e30))
    top = jnp.max(raw, axis=1, keepdims=True)
    probs = jnp.exp2((raw - top) * jnp.float32(COEF))
    return probs.astype(jnp.bfloat16), jnp.sum(probs, axis=1, keepdims=True)


def attend_units(kv, units):
    raws = []
    for qblk, listed, _ in units:
        kcat = jnp.concatenate([kv[0, e] for e in listed], axis=0)
        raws.append(lax.dot_general(qblk, kcat, (((1,), (1,)), ((), ())), preferred_element_type=jnp.float32))
    soft = [soften(raw, block) for raw, (_, _, block) in zip(raws, units)]
    done = []
    for (probs, total), (_, listed, _) in zip(soft, units):
        vcat = jnp.concatenate([kv[1, e] for e in listed], axis=0)
        done.append((jnp.dot(probs, vcat, preferred_element_type=jnp.float32) / total).astype(jnp.bfloat16))
    return done


def kernel(nc, nt, ratio, mult, lists, q, k, v, out, qh, kv, oh,
           s_kv, s_q, s_o, s_f, s_s, l_kv, l_o, r_kv, r_f, r_s, r_q, r_o):
    n = nc * nt
    rows = q.shape[0]
    per = rows // BLK
    c, t = lax.axis_index("seq"), lax.axis_index("tensor")
    me = c * nt + t
    sib = 1 - t

    def dev(chip, core):
        return {"seq": chip, "tensor": core}

    def part(index):
        return pl.ds(pl.multiple_of(index * rows, rows), rows)

    def blocks(index):
        return pl.ds(index * per, per)

    def cols(head):
        return pl.ds(pl.multiple_of(head * HD, HD), HD)

    def remote(src, dst, send, recv, chip, core):
        return pltpu.make_async_remote_copy(
            src_ref=src, dst_ref=dst, send_sem=send, recv_sem=recv,
            device_id=dev(chip, core), device_id_type=MESH,
        )

    def drain(ref, sem):
        pltpu.make_async_copy(ref, ref, sem).wait()

    def loop(start, stop, step):
        def run(i, _):
            step(i)
            return 0
        lax.fori_loop(start, stop, run, 0)

    barrier = pltpu.get_barrier_semaphore()

    def greet(i):
        p = lax.rem(me + i, n)
        pl.semaphore_signal(barrier, inc=1, device_id=dev(p // nt, lax.rem(p, nt)), device_id_type=MESH)

    loop(1, n, greet)
    pl.semaphore_wait(barrier, n - 1)

    def send_kv(j):
        dc = lax.rem(c + j * mult, nc)
        head = cols((dc * nt) // ratio)
        for core, src in ((0, k), (1, v)):
            remote(src.at[:, :, head], kv.at[core, blocks(me)], s_kv, r_kv.at[me], dc, core).start()

    loop(1, nc, send_kv)
    head = cols(me // ratio)
    local = []
    for core, src in ((0, k), (1, v)):
        remote(src.at[:, :, head], kv.at[core, blocks(me)], s_s.at[core], r_s.at[core], c, sib).start()
        local.append(pltpu.make_async_copy(src.at[:, :, head], kv.at[core, blocks(me)], l_kv.at[core]))
        local[-1].start()

    pltpu.make_async_copy(q.at[:, cols(me)], qh.at[part(me)], r_q.at[me]).start()
    remote(q.at[:, cols(c * nt + sib)], qh.at[part(me)], s_q, r_q.at[me], c, sib).start()

    def send_q(j):
        dc = lax.rem(c + j * mult, nc)
        for core in range(nt):
            remote(q.at[:, cols(dc * nt + core)], qh.at[part(me)], s_q, r_q.at[me], dc, core).start()

    loop(1, nc, send_q)

    def forward(j):
        sc = lax.rem(c + (nc - j) * mult, nc)
        for core in range(nt):
            s = sc * nt + core
            drain(kv.at[t, blocks(s)], r_kv.at[s])
            remote(kv.at[t, blocks(s)], kv.at[t, blocks(s)], s_f, r_f, c, sib).start()

    loop(1, nc, forward)
    for core in range(nt):
        local[core].wait()
        drain(kv.at[core, blocks(0)], r_s.at[core])
    drain(kv.at[0, pl.ds(0, (n - nt) * per)], r_f)

    def attend(i):
        j = i // nt
        sc = lax.rem(c + (nc - j) * mult, nc)
        score = lax.rem(t + i, nt)
        s = sc * nt + score
        drain(qh.at[part(s)], r_q.at[s])
        units, places = [], []
        for inner in range(per):
            block = s * per + inner
            places.append(pl.ds(pl.multiple_of(block * BLK, BLK), BLK))
            units.append((qh[places[-1], :], [lists[block * KSEL + e] for e in range(KSEL)], block))
        for here, made in zip(places, attend_units(kv, units)):
            oh[here, :] = made

        @pl.when(i == 0)
        def _():
            pltpu.make_async_copy(oh.at[part(s)], out.at[:, cols(me)], l_o).start()

        @pl.when(i > 0)
        def _():
            remote(oh.at[part(s)], out.at[:, cols(me)], s_o, r_o, sc, score).start()

    loop(0, n, attend)

    drain(oh.at[part(0)], l_o)
    others = pl.ds(0, (n - 1) * HD)
    drain(out.at[:, others], r_o)
    drain(out.at[:, others], s_o)
    drain(out.at[:, others], s_q)
    drain(kv.at[0, pl.ds(0, (n - nt) * per)], s_kv)
    drain(kv.at[0, pl.ds(0, (n - nt) * per)], s_f)
    for core in range(nt):
        drain(kv.at[core, blocks(0)], s_s.at[core])


def halves_kernel(nc, lists, q, k, v, out, lv, ls, qh, kva, kvb, oh,
                  s_l, r_l, c_l, s_own, s_up, s_q, s_o, s_f, s_s, l_kv, r_kv, r_f, r_s, r_q, r_o):
    nt = 2
    n = nc * nt
    half = nc // 2
    row = half // 2
    rows = q.shape[0]
    per = rows // BLK
    kvs = (kva, kvb)
    c, t = lax.axis_index("seq"), lax.axis_index("tensor")
    me = c * nt + t
    sib = 1 - t
    hz, cx = c // half, lax.rem(c, half)
    base = hz * half
    tz = cx // row
    mine = lax.rem(cx, row) * nt + t

    def dev(chip, core):
        return {"seq": chip, "tensor": core}

    def blocks(index):
        return pl.ds(index * per, per)

    def cols(index, width):
        return pl.ds(pl.multiple_of(index * width, width), width)

    def remote(src, dst, send, recv, chip, core):
        return pltpu.make_async_remote_copy(
            src_ref=src, dst_ref=dst, send_sem=send, recv_sem=recv,
            device_id=dev(chip, core), device_id_type=MESH,
        )

    def drain(ref, sem):
        pltpu.make_async_copy(ref, ref, sem).wait()

    def loop(start, stop, step):
        def run(i, _):
            step(i)
            return 0
        lax.fori_loop(start, stop, run, 0)

    barrier = pltpu.get_barrier_semaphore()

    def greet(i):
        p = lax.rem(me + i, n)
        pl.semaphore_signal(barrier, inc=1, device_id=dev(p // nt, lax.rem(p, nt)), device_id_type=MESH)

    loop(1, n, greet)
    pl.semaphore_wait(barrier, n - 1)

    def send_kv(j, dc, sem):
        at = cols((lax.rem(dc, half)) * 2 + j, HD)
        for core, src in ((0, k), (1, v)):
            remote(src.at[:, :, at], kvs[j].at[core, blocks(me)], sem, r_kv.at[j, me], dc, core).start()

    def send_up(j):
        @pl.when(hz == 0)
        def _():
            loop(0, half, lambda i: send_kv(j, half + lax.rem(cx + i, half), s_up))

    def send_own(j):
        loop(1, half, lambda i: send_kv(j, base + lax.rem(cx + i, half), s_own))
        at = cols(cx * 2 + j, HD)
        for core, src in ((0, k), (1, v)):
            remote(src.at[:, :, at], kvs[j].at[core, blocks(me)], s_s.at[j, core], r_s.at[j, core], c, sib).start()
            pltpu.make_async_copy(src.at[:, :, at], kvs[j].at[core, blocks(me)], l_kv.at[j, core]).start()

    entry = lax.rem(me, 4)
    for far in range(2):
        dc = far * half + me // 4
        for core in range(nt):
            itself = (dc == c) & (t == core)

            @pl.when(itself)
            def _():
                pltpu.make_async_copy(lists, lv.at[entry], r_l.at[entry]).start()

            @pl.when(jnp.logical_not(itself))
            def _():
                remote(lists, lv.at[entry], s_l.at[far, core], r_l.at[entry], dc, core).start()

    send_own(0)

    def send_q(i):
        cl = lax.rem(cx + i, half)
        remote(q.at[:, cols(cl, 4 * HD)], qh.at[mine], s_q, r_q.at[mine], base + cl, tz).start()

    @pl.when(tz == t)
    def _():
        pltpu.make_async_copy(q.at[:, cols(cx, 4 * HD)], qh.at[mine], r_q.at[mine]).start()

    @pl.when(tz != t)
    def _():
        send_q(0)

    loop(1, half, send_q)
    send_own(1)
    send_up(0)
    send_up(1)

    def forward(j, chip):
        for core in range(nt):
            here = kvs[j].at[t, blocks(chip * nt + core)]
            drain(here, r_kv.at[j, chip * nt + core])
            remote(here, here, s_f.at[j], r_f.at[j], c, sib).start()

    def forward_own(j):
        loop(1, half, lambda i: forward(j, base + lax.rem(cx + half - i, half)))

    def settle(j):
        for core in range(nt):
            drain(kvs[j].at[core, blocks(0)], r_s.at[j, core])
            drain(kvs[j].at[core, blocks(0)], l_kv.at[j, core])

        @pl.when(hz == 0)
        def _():
            drain(kvs[j].at[0, pl.ds(0, (half - 1) * nt * per)], r_f.at[j])

        @pl.when(hz == 1)
        def _():
            drain(kvs[j].at[0, pl.ds(0, (nc - 1) * nt * per)], r_f.at[j])

    forward_own(0)

    @pl.when(hz == 1)
    def _():
        loop(0, half, lambda i: forward(0, lax.rem(cx + half - i, half)))

    for e in range(4):
        drain(lv.at[e], r_l.at[e])
    pltpu.make_async_copy(lv, ls, c_l).start()
    settle(0)
    pltpu.make_async_copy(lv, ls, c_l).wait()

    def attend(j, i):
        slot = lax.rem(mine // nt + 1 + i // nt, 2) * nt + lax.rem(t + i, nt)
        sc, score = base + t * row + slot // nt, lax.rem(slot, nt)
        if j == 0:
            drain(qh.at[slot], r_q.at[slot])
        units, places = [], []
        for inner in range(per):
            block = (sc * nt + score) * per + inner
            for one in range(2):
                head = 2 * j + one
                listed = [ls[head, e, 0, block] for e in range(KSEL)]
                here = pl.ds(inner * BLK, BLK)
                places.append((here, pl.ds(one * HD, HD)))
                units.append((qh[slot, here, pl.ds(head * HD, HD)], listed, block))
        for here, made in zip(places, attend_units(kvs[j], units)):
            oh[slot, j, here[0], here[1]] = made
        itself = (sc == c) & (score == t)
        goal = out.at[:, cols(cx * 2 + j, 2 * HD)]

        @pl.when(itself)
        def _():
            pltpu.make_async_copy(oh.at[slot, j], goal, r_o.at[cx, j]).start()

        @pl.when(jnp.logical_not(itself))
        def _():
            remote(oh.at[slot, j], goal, s_o, r_o.at[cx, j], sc, score).start()

    def first(i):
        @pl.when(i == 0)
        def _():
            forward_own(1)

        attend(0, i)

        @pl.when(hz == 1)
        def _():
            forward(1, lax.rem(cx + half - i, half))

    loop(0, 4, first)
    settle(1)
    loop(0, 4, lambda i: attend(1, i))

    for cl in range(half):
        for j in range(2):
            drain(out.at[:, pl.ds((cl * 2 + j) * 2 * HD, 2 * HD)], r_o.at[cl, j])

    @pl.when(tz == t)
    def _():
        drain(out.at[:, pl.ds(0, 3 * 4 * HD)], s_q)

    @pl.when(tz != t)
    def _():
        drain(out, s_q)

    @pl.when((base + t * row == c - lax.rem(cx, row)))
    def _():
        drain(out.at[:, pl.ds(0, 6 * 2 * HD)], s_o)

    @pl.when((base + t * row != c - lax.rem(cx, row)))
    def _():
        drain(out, s_o)

    drain(kva.at[0, pl.ds(0, (half - 1) * 4 * per)], s_own)

    @pl.when(hz == 0)
    def _():
        drain(kva.at[0], s_up)

    for j in range(2):
        @pl.when(hz == 0)
        def _():
            drain(kva.at[0, pl.ds(0, (half - 1) * nt * per)], s_f.at[j])

        @pl.when(hz == 1)
        def _():
            drain(kva.at[0, pl.ds(0, (nc - 1) * nt * per)], s_f.at[j])

        for core in range(nt):
            drain(kva.at[core, blocks(0)], s_s.at[j, core])

    for far in range(2):
        dc = far * half + me // 4
        for core in range(nt):
            @pl.when(jnp.logical_not((dc == c) & (t == core)))
            def _():
                drain(lv.at[0], s_l.at[far, core])


def halves(nc, queries, keys, values, block_lists):
    rows, width = queries.shape
    n = 2 * nc
    per = rows // BLK
    dma = pltpu.SemaphoreType.DMA
    hbm = pl.BlockSpec(memory_space=pl.ANY)
    entry = (KSEL, 1, block_lists.shape[1])
    kv = pltpu.VMEM((2, n * per, BLK, HD), jnp.bfloat16)
    return pl.pallas_call(
        functools.partial(halves_kernel, nc),
        out_shape=pltpu.VMEM((rows, width), jnp.bfloat16),
        in_specs=[hbm, hbm, hbm, hbm],
        out_specs=hbm,
        scratch_shapes=[
            pltpu.VMEM((4, *entry), jnp.int32),
            pltpu.SMEM((4, *entry), jnp.int32),
            pltpu.VMEM((4, rows, 4 * HD), jnp.bfloat16),
            kv,
            kv,
            pltpu.VMEM((4, 2, rows, 2 * HD), jnp.bfloat16),
            dma((2, 2)), dma((4,)), dma, dma, dma, dma, dma, dma((2,)), dma((2, 2)), dma((2, 2)),
            dma((2, n)), dma((2,)), dma((2, 2)), dma((4,)), dma((nc // 2, 2)),
        ],
        compiler_params=pltpu.CompilerParams(
            collective_id=0, has_side_effects=True, vmem_limit_bytes=VMEM_MIB * 2**20
        ),
        cost_estimate=pl.CostEstimate(
            flops=4 * n * rows * KSEL * BLK * HD, bytes_accessed=8 * n * rows * HD, transcendentals=n * rows * KSEL * BLK
        ),
    )(block_lists.transpose(2, 0, 1), queries, keys.reshape(per, BLK, -1), values.reshape(per, BLK, -1))


def body(nc, nt, queries, keys, values, block_lists):
    rows, width = queries.shape
    n = nc * nt
    heads = width // HD
    kv_heads = keys.shape[1] // HD
    ratio = heads // kv_heads
    assert nt == 2 and heads == n and ratio % nt == 0 and rows % BLK == 0
    if nc == 8 and ratio == 2:
        return halves(nc, queries, keys, values, block_lists)
    mult = nc // 2 - 1 if nc >= 4 and nc & (nc - 1) == 0 else 1
    dma, shape = pltpu.SemaphoreType.DMA, jax.ShapeDtypeStruct
    hbm = pl.BlockSpec(memory_space=pl.ANY)
    return pl.pallas_call(
        functools.partial(kernel, nc, nt, ratio, mult),
        out_shape=shape((rows, width), jnp.bfloat16),
        in_specs=[pl.BlockSpec(memory_space=pltpu.SMEM), hbm, hbm, hbm],
        out_specs=hbm,
        scratch_shapes=[
            pltpu.VMEM((n * rows, HD), jnp.bfloat16),
            pltpu.VMEM((2, n * rows // BLK, BLK, HD), jnp.bfloat16),
            pltpu.VMEM((n * rows, HD), jnp.bfloat16),
            dma, dma, dma, dma, dma((nt,)), dma((nt,)), dma,
            dma((n,)), dma, dma((nt,)), dma((n,)), dma,
        ],
        compiler_params=pltpu.CompilerParams(
            collective_id=0, has_side_effects=True, vmem_limit_bytes=40 * 2**20
        ),
        cost_estimate=pl.CostEstimate(
            flops=4 * n * rows * KSEL * BLK * HD, bytes_accessed=8 * n * rows * HD, transcendentals=n * rows * KSEL * BLK
        ),
    )(
        block_lists.reshape(-1),
        queries,
        keys.reshape(rows // BLK, BLK, kv_heads * HD),
        values.reshape(rows // BLK, BLK, kv_heads * HD),
    )


def solution(mesh):
    placed = (
        P(("groups", "seq", "tensor"), None),
        P(("groups", "seq", "tensor"), None),
        P(("groups", "seq", "tensor"), None),
        P(("seq", "tensor"), None, None),
    )
    return jax.shard_map(
        functools.partial(body, mesh.shape["seq"], mesh.shape["tensor"]),
        mesh=mesh,
        in_specs=placed,
        out_specs=P(("groups", "seq", "tensor"), None),
        check_vma=False,
    )
```
